256 devices in a mesh: gx: 64 (over y_hi, x, z), gy: 4 (over y_lo, core).
Axes of the slice: x: 4, y: 4 (y_hi: 2, y_lo: 2; y = y_hi * 2 + y_lo), z: 8, core: 2. Of those that a mesh axis runs over, the one named last changes fastest.
Arguments:
- acid_field: float32 [8, 1024, 16384], P(None, 'gy', 'gx'), may hold values from 0 to 1
- quencher_field: float32 [8, 1024, 16384], P(None, 'gy', 'gx'), may hold values from 0.1 to 0.5
Outputs:
- acid_after: float32 [8, 1024, 16384], P(None, 'gy', 'gx')
- inhibitor: float32 [8, 1024, 16384], P(None, 'gy', 'gx')
- etch_rate: float32 [1024, 16384], P('gy', 'gx')
The draws below stay inside these ranges and needn't reach their ends.
All inputs are finite; a program needn't handle non-finite values.
Results may differ from the reference program's by a relative error of at most 0.00005.
Values sent between devices are 32-bit elements; how exact they have to be, the bound alone decides.
No kernel may reach another device: no remote copies, remote signals or barrier semaphores. Data moves between devices by JAX's collectives and lax.ppermute only.
A program may use at most 128 MiB of HBM per device.

```python
import jax
import jax.numpy as jnp
from jax import lax

TILE = 256
DEPTH = 8
STEPS = 4
COARSEN = 8
NR = 1024
NC = 16384


def block_levels(rng, extent, split, least, largest):
    factor_of, own = 1.0, jax.random.fold_in(rng, 6)
    for dim, parts in split:
        draws = jnp.exp(jax.random.uniform(jax.random.fold_in(own, dim), (parts,), jnp.float32, least / len(split), largest / len(split)))
        factor_of = factor_of * jnp.repeat(draws, extent[dim] // parts).reshape([-1 if axis == dim else 1 for axis in range(len(extent))])
    return factor_of


def setup_inputs(seed: int = 0) -> dict:
    key_of = jax.random.split(jax.random.key(seed), 3)
    acid_field = jnp.clip(1.0 * jax.random.uniform(key_of[0], (DEPTH, NR, NC), jnp.float32) ** block_levels(key_of[0], (DEPTH, NR, NC), ((1, 4), (2, 64)), -0.2, 0.2), 0.0, 1.0)
    quencher_field = jnp.clip(0.1 + 0.4 * jax.random.uniform(key_of[1], (DEPTH, NR, NC), jnp.float32) ** block_levels(key_of[1], (DEPTH, NR, NC), ((1, 4), (2, 64)), -0.2, 0.2), 0.1, 0.5)
    return dict(acid_field=acid_field, quencher_field=quencher_field)


RATE_ACID = 0.15
RATE_QUENCH = 0.05
NEUTRAL = 0.1
DEPROTECT = 0.35
LOADING = 0.8


def neighbours(field):
    padded = jnp.pad(field, ((0, 0), (1, 1), (1, 1)))
    lateral = padded[:, 2:, 1:-1] + padded[:, :-2, 1:-1] + padded[:, 1:-1, 2:] + padded[:, 1:-1, :-2]
    vertical = jnp.concatenate([field[:1], field[:-1]], 0) + jnp.concatenate([field[1:], field[-1:]], 0)
    return lateral + vertical - 6.0 * field


def kernel(distance, coarse_tile):
    spread = 25.0 * coarse_tile / 32.0
    offset_float = distance.astype(jnp.float32)
    return jnp.where(jnp.abs(distance) <= 2 * coarse_tile, jnp.exp(-offset_float * offset_float / (2.0 * spread * spread)), 0.0)


def reference(acid_field, quencher_field):
    acid_now = acid_field
    quench_now = quencher_field
    inhibitor = jnp.ones_like(acid_field)
    for step in range(STEPS):
        reaction = NEUTRAL * acid_now * quench_now
        new_acid = acid_now + RATE_ACID * neighbours(acid_now) - reaction
        new_quench = quench_now + RATE_QUENCH * neighbours(quench_now) - reaction
        inhibitor = inhibitor * jnp.exp(-DEPROTECT * acid_now)
        acid_now = new_acid
        quench_now = new_quench
    coarse_tile = TILE // COARSEN
    coarse_rows = NR // COARSEN
    coarse_cols = NC // COARSEN
    density = (1.0 - inhibitor).reshape(DEPTH, coarse_rows, COARSEN, coarse_cols, COARSEN).mean(axis=(0, 2, 4))
    kernel_total = jnp.sum(kernel(jnp.arange(-2 * coarse_tile, 2 * coarse_tile + 1), coarse_tile))
    col_index = jnp.arange(coarse_cols)
    col_band = kernel(col_index[:, None] - col_index[None, :], coarse_tile)
    across = jnp.dot(density, col_band, precision=lax.Precision.HIGHEST) / kernel_total
    row_index = jnp.arange(coarse_rows)
    row_band = kernel(row_index[None, :] - row_index[:, None], coarse_tile)
    smoothed = jnp.dot(row_band, across, precision=lax.Precision.HIGHEST) / kernel_total
    fine_map = jnp.repeat(jnp.repeat(smoothed, COARSEN, 0), COARSEN, 1)
    etch_rate = (1.0 - inhibitor[0]) * (1.0 - LOADING * fine_map)
    return acid_now, inhibitor, etch_rate
```

```python
import jax
import jax.numpy as jnp
import numpy as np
from jax import lax
from jax.experimental import pallas as pl
from jax.experimental.pallas import tpu as pltpu
from jax.sharding import PartitionSpec as P

RATE_ACID = 0.15
RATE_QUENCH = 0.05
NEUTRAL = 0.1
DEPROTECT = 0.35
LOADING = 0.8
STEPS = 4
COARSEN = 8
REACH = 64
SPREAD = 25.0

LAYERS = 8
ROWS = 256
COLS = 256
LANES = 128
SUBS = 8
RUN = ROWS // SUBS
HALO = STEPS
EXT = RUN + 2 * HALO
FOLD = EXT // 2
TILE = ROWS // COARSEN

VM = pl.BlockSpec(memory_space=pltpu.VMEM)
HB = pl.BlockSpec(memory_space=pltpu.HBM)
F32 = jnp.float32


def params(mib):
    return pltpu.CompilerParams(vmem_limit_bytes=mib * 1024 * 1024)


def vmem(shape):
    return pltpu.VMEM(shape, F32)


def iota(dim):
    return lax.broadcasted_iota(jnp.int32, (SUBS, LANES), dim)


def row_strips(a_top, a_bot, q_top, q_bot, first_ref, second_ref):
    even = lax.rem(lax.axis_index("gy"), 2) == 0
    low = lax.broadcasted_iota(jnp.int32, (SUBS, COLS), 0) < HALO
    for d in range(LAYERS):
        top = jnp.where(low, a_top[d], pltpu.roll(q_top[d], HALO, 0))
        bot = jnp.where(low, pltpu.roll(a_bot[d], HALO, 0), q_bot[d])
        first_ref[d] = jnp.where(even, bot, top)
        second_ref[d] = jnp.where(even, top, bot)


def pack_rows(acid, quench):
    block = (LAYERS, SUBS, COLS)
    top = pl.BlockSpec(block, lambda i: (0, 0, 0))
    bot = pl.BlockSpec(block, lambda i: (0, RUN - 1, 0))
    out = jax.ShapeDtypeStruct(block, F32)
    return pl.pallas_call(
        row_strips,
        grid=(1,),
        in_specs=[top, bot, top, bot],
        out_specs=[pl.BlockSpec(block, lambda i: (0, 0, 0))] * 2,
        out_shape=[out, out],
        compiler_params=params(4),
        name="pack_rows",
    )(acid, acid, quench, quench)


def spread_rows(acid, quench, state, land, sems):
    copies = []
    for d in range(LAYERS):
        for t in range(4):
            source = (acid, quench)[t // 2].at[d, :, pl.ds((t % 2) * LANES, LANES)]
            copy = pltpu.make_async_copy(source, land.at[d, t], sems.at[d, t])
            copy.start()
            copies.append(copy)
    for d in range(LAYERS):
        for t in range(4):
            copies[d * 4 + t].wait()
            for k in range(RUN):
                state[t, d, HALO + k] = land[d, t, pl.ds(k, SUBS, stride=RUN), :]


def load_state(acid, quench):
    return pl.pallas_call(
        spread_rows,
        in_specs=[HB, HB],
        out_specs=VM,
        out_shape=vmem((4, LAYERS, EXT, SUBS, LANES)),
        scratch_shapes=[
            pltpu.VMEM((LAYERS, 4, ROWS, LANES), F32),
            pltpu.SemaphoreType.DMA((LAYERS, 4)),
        ],
        compiler_params=params(8),
        name="load_state",
    )(acid, quench)


def column_strips(state_in, first_in, second_in, state, first_ref, second_ref):
    del state_in
    even_row = lax.rem(lax.axis_index("gy"), 2) == 0
    even_col = lax.rem(lax.axis_index("gx"), 2) == 0
    sub = iota(0)
    lane = iota(1)
    for d in range(LAYERS):
        for t in range(2):
            cols = pl.ds(t * LANES, LANES)
            one, two = first_in[d, :, cols], second_in[d, :, cols]
            top = jnp.where(even_row, two, one)
            bot = jnp.where(even_row, one, two)
            for f in range(2):
                for j in range(HALO):
                    row = f * HALO + j
                    above = pltpu.roll(state[2 * f + t, d, HALO + RUN - HALO + j], 1, 0)
                    edge = pltpu.roll(top, (SUBS - row) % SUBS, 0)
                    state[2 * f + t, d, j] = jnp.where(sub == 0, edge, above)
                    below = pltpu.roll(state[2 * f + t, d, HALO + j], SUBS - 1, 0)
                    edge = pltpu.roll(bot, SUBS - 1 - row, 0)
                    state[2 * f + t, d, HALO + RUN + j] = jnp.where(sub == SUBS - 1, edge, below)

    def gather(k, _):
        left = jnp.zeros((SUBS, LANES), F32)
        right = jnp.zeros((SUBS, LANES), F32)
        for half in range(2):
            for f in range(2):
                for d in range(LAYERS):
                    at = 64 * f + 32 * half + HALO * d
                    here = (lane >= at) & (lane < at + HALO)
                    first = state[2 * f, d, k + FOLD * half]
                    last = state[2 * f + 1, d, k + FOLD * half]
                    left = jnp.where(here, pltpu.roll(first, at, 1), left)
                    right = jnp.where(here, pltpu.roll(last, (at + HALO) % LANES, 1), right)
        first_ref[k] = jnp.where(even_col, right, left)
        second_ref[k] = jnp.where(even_col, left, right)
        return 0

    lax.fori_loop(0, FOLD, gather, 0)


def pack_columns(state, first, second):
    strip = jax.ShapeDtypeStruct((FOLD, SUBS, LANES), F32)
    return pl.pallas_call(
        column_strips,
        in_specs=[VM, VM, VM],
        out_specs=[VM, VM, VM],
        out_shape=[vmem((4, LAYERS, EXT, SUBS, LANES)), strip, strip],
        input_output_aliases={0: 0},
        compiler_params=params(4),
        name="pack_columns",
    )(state, first, second)


def shifted(x, by):
    return pltpu.roll(x, by % LANES, 1)


def sides(lane, before, x, after):
    return jnp.where(lane == 0, before, shifted(x, 1)) + jnp.where(
        lane == LANES - 1, after, shifted(x, -1)
    )


def bake(state, first_in, second_in, out, edge_out, guard, density, one, two, edge_a, edge_b, total, pooled, coef):
    gx, gy = lax.axis_index("gx"), lax.axis_index("gy")
    even_col = lax.rem(gx, 2) == 0
    lane, sub = iota(1), iota(0)
    at_left = ((lane >= 96) | ((lane >= 32) & (lane < 64)))
    is_acid = (lane < 32) | (lane >= 96)
    wall = jnp.where(at_left, (gx == 0).astype(jnp.int32), (gx == lax.axis_size("gx") - 1).astype(jnp.int32))
    lanes_open = 1.0 - wall.astype(F32)
    for c in range(3):
        closed = jnp.zeros((SUBS, LANES), jnp.int32)
        if c == 0:
            closed = jnp.where(sub == 0, (gy == 0).astype(jnp.int32), 0)
        if c == 2:
            closed = jnp.where(sub == SUBS - 1, (gy == lax.axis_size("gy") - 1).astype(jnp.int32), 0)
        is_open = 1.0 - closed.astype(F32)
        coef[c, 0] = RATE_ACID * is_open
        coef[c, 1] = NEUTRAL * is_open
        coef[c, 2] = RATE_QUENCH * is_open
        coef[c, 3] = (1.0 - 6.0 * RATE_QUENCH) * is_open
        coef[c, 4] = jnp.where(is_acid, RATE_ACID, RATE_QUENCH) * is_open * lanes_open
        coef[c, 5] = NEUTRAL * is_open * lanes_open

    def unpack(k, _):
        a, b = first_in[k], second_in[k]
        left = jnp.where(even_col, b, a)
        right = jnp.where(even_col, a, b)
        for half in range(2):
            for d in range(LAYERS):
                at = 32 * half + HALO * d
                edge_a[d, k + FOLD * half] = jnp.where(
                    at_left, shifted(left, -at - HALO), shifted(right, -at)
                )
        return 0

    lax.fori_loop(0, FOLD, unpack, 0)
    ratio = jnp.where(is_acid, 1.0, (1.0 - 6.0 * RATE_QUENCH) / NEUTRAL)

    def advance(src, src_edge, dst, dst_edge, k, kind, visit):
        c15, c10, c05, c07 = (coef[kind, i] for i in range(4))
        cs, ct = coef[kind, 4], coef[kind, 5]
        load = lambda d, j: [src[t, d, j] for t in range(4)] + [src_edge[d, j]]
        before = center = load(0, k)
        for d in range(LAYERS):
            after = load(d + 1, k) if d + 1 < LAYERS else center
            up, down = load(d, k - 1), load(d, k + 1)
            a0, a1, q0, q1, e = center
            ra0, ra1, re = shifted(a0, 1), shifted(a1, 1), shifted(e, 1)
            la0, la1, le = shifted(a0, -1), shifted(a1, -1), shifted(e, -1)
            rq0, lq1 = shifted(q0, 1), shifted(q1, -1)
            across = [
                jnp.where(lane == 0, re, ra0) + jnp.where(lane == LANES - 1, la1, la0),
                jnp.where(lane == 0, ra0, ra1) + jnp.where(lane == LANES - 1, le, la1),
                jnp.where(lane == 0, shifted(e, 65), rq0)
                + jnp.where(lane == LANES - 1, lq1, shifted(q0, -1)),
                jnp.where(lane == 0, rq0, shifted(q1, 1))
                + jnp.where(lane == LANES - 1, shifted(e, 63), lq1),
                jnp.where(lane == 0, ra1, jnp.where(lane == 64, shifted(q1, 65), re))
                + jnp.where(lane == LANES - 1, la0, jnp.where(lane == 63, shifted(q0, 63), le)),
            ]
            around = [
                (up[i] + down[i]) + (before[i] + after[i]) + across[i] for i in range(5)
            ]
            for t in range(2):
                scaled = c10 * center[t]
                acid = c15 * around[t] + scaled * (1.0 - center[2 + t])
                dst[t, d, k] = acid
                dst[2 + t, d, k] = c05 * around[2 + t] + center[2 + t] * (c07 - scaled)
                visit(t, d, k, center[t], acid)
            dst_edge[d, k] = cs * around[4] + ct * e * (ratio - shifted(e, 64))
            before, center = center, after

    def sweep(src, src_edge, dst, dst_edge, margin, visit):
        def outer(kind):
            def body(k, _):
                advance(src, src_edge, dst, dst_edge, k, kind, lambda *_: None)
                return 0

            return body

        def inner(k, _):
            advance(src, src_edge, dst, dst_edge, k, 1, visit)
            return 0

        lax.fori_loop(HALO - margin, HALO, outer(0), 0)
        lax.fori_loop(HALO, HALO + RUN, inner, 0)
        lax.fori_loop(HALO + RUN, HALO + RUN + margin, outer(2), 0)

    def begin(t, d, k, old, new):
        total[t, d, k - HALO] = old + new

    sweep(state, edge_a, one, edge_b, 3, begin)
    sweep(one, edge_b, two, edge_a, 2, lambda *_: None)

    def protect(t, d, k, old, new):
        left = jnp.exp(-DEPROTECT * (total[t, d, k - HALO] + (old + new)))
        guard[t, d, k - HALO] = left
        pooled[t, k - HALO] = left if d == 0 else pooled[t, k - HALO] + left

    sweep(two, edge_a, out, edge_out, 1, protect)

    fine = jnp.concatenate(
        [
            jnp.concatenate(
                [sum(pooled[t, COARSEN * g + i] for i in range(COARSEN)) for t in range(2)], 1
            )
            for g in range(RUN // COARSEN)
        ],
        0,
    )
    col = lax.broadcasted_iota(jnp.int32, (COLS, LANES), 0)
    block = lax.broadcasted_iota(jnp.int32, (COLS, LANES), 1)
    pool = (col // COARSEN == block).astype(F32)
    sums = jnp.dot(fine, pool, precision=lax.Precision.HIGHEST, preferred_element_type=F32)
    wide = lax.broadcasted_iota(jnp.int32, (TILE, LANES), 1)
    mean = 1.0 - sums * (1.0 / (LAYERS * COARSEN * COARSEN))
    density[...] = jnp.where(wide < TILE, mean, 0.0)


def run_bake(state, first, second):
    grid = (4, LAYERS, EXT, SUBS, LANES)
    edge = (LAYERS, EXT, SUBS, LANES)
    half = (2, LAYERS, RUN, SUBS, LANES)
    return pl.pallas_call(
        bake,
        in_specs=[VM] * 3,
        out_specs=[VM] * 4,
        out_shape=[vmem(grid), vmem(edge), vmem(half), jax.ShapeDtypeStruct((TILE, LANES), F32)],
        scratch_shapes=[
            pltpu.VMEM(grid, F32),
            pltpu.VMEM(grid, F32),
            pltpu.VMEM(edge, F32),
            pltpu.VMEM(edge, F32),
            pltpu.VMEM(half, F32),
            pltpu.VMEM((2, RUN, SUBS, LANES), F32),
            pltpu.VMEM((3, 6, SUBS, LANES), F32),
        ],
        compiler_params=params(20),
        name="bake",
    )(state, first, second)


def last_step(state, edge, guard, acid_out, guard_out, bare, land_a, land_m, sems):
    lane = iota(1)
    copies = []
    for d in range(LAYERS):
        low, high = max(d - 1, 0), min(d + 1, LAYERS - 1)

        def body(k, _, d=d, low=low, high=high):
            j = k + HALO
            e = edge[d, j]
            a0, a1 = state[0, d, j], state[1, d, j]
            ra0, la1 = shifted(a0, 1), shifted(a1, -1)
            across = [
                jnp.where(lane == 0, shifted(e, 1), ra0)
                + jnp.where(lane == LANES - 1, la1, shifted(a0, -1)),
                jnp.where(lane == 0, ra0, shifted(a1, 1))
                + jnp.where(lane == LANES - 1, shifted(e, -1), la1),
            ]
            for t, a in enumerate((a0, a1)):
                around = (
                    (state[t, d, j - 1] + state[t, d, j + 1])
                    + (state[t, low, j] + state[t, high, j])
                    + across[t]
                )
                rows = pl.ds(k, SUBS, stride=RUN)
                land_a[d, t, rows, :] = RATE_ACID * around + (NEUTRAL * a) * (
                    1.0 - state[2 + t, d, j]
                )
                left = guard[t, d, k]
                land_m[d, t, rows, :] = left
                if d == 0:
                    bare[t, rows, :] = 1.0 - left
            return 0

        lax.fori_loop(0, RUN, body, 0, unroll=4)
        for t in range(2):
            for i, (land, target) in enumerate(((land_a, acid_out), (land_m, guard_out))):
                copy = pltpu.make_async_copy(
                    land.at[d, t], target.at[d, :, pl.ds(t * LANES, LANES)], sems.at[d, t, i]
                )
                copy.start()
                copies.append(copy)
    for copy in copies:
        copy.wait()


def run_last(state, edge, guard):
    whole = jax.ShapeDtypeStruct((LAYERS, ROWS, COLS), F32)
    return pl.pallas_call(
        last_step,
        in_specs=[VM] * 3,
        out_specs=[HB, HB, VM],
        out_shape=[whole, whole, vmem((2, ROWS, LANES))],
        scratch_shapes=[
            pltpu.VMEM((LAYERS, 2, ROWS, LANES), F32),
            pltpu.VMEM((LAYERS, 2, ROWS, LANES), F32),
            pltpu.SemaphoreType.DMA((LAYERS, 2, 2)),
        ],
        compiler_params=params(8),
        name="last_step",
    )(state, edge, guard)


def weights(distance):
    offset = np.arange(-REACH, REACH + 1, dtype=np.float64)
    norm = np.exp(-offset * offset / (2.0 * SPREAD * SPREAD)).sum()
    value = np.exp(-(distance.astype(np.float64) ** 2) / (2.0 * SPREAD * SPREAD))
    return np.where(np.abs(distance) <= REACH, value / norm, 0.0).astype(np.float32)


def row_table():
    p = np.arange(TILE)
    coarse = (p % SUBS) * (TILE // SUBS) + p // SUBS
    me = np.arange(4)[:, None, None, None]
    k = np.arange(4)[None, None, :, None]
    i = np.arange(TILE)[None, :, None, None]
    distance = TILE * ((me ^ k) - me) + coarse[None, None, None, :] - i
    return weights(distance).reshape(4, TILE, 4 * TILE)


def column_table():
    c = np.arange(7 * TILE)[:, None] - 3 * TILE
    return weights(c - np.arange(COLS)[None, :] // COARSEN)


def etch(own, mate, near, far, bare, row_ref, col_ref, out, grid, cols):
    gx, gy = lax.axis_index("gx"), lax.axis_index("gy")
    odd = lax.rem(gx, 2)
    upper = lax.rem(lax.div(gx, 2), 2)
    swap = 1 - 2 * odd
    step = 2 - 4 * upper
    tiles = [own[...], mate[...], near[0], near[1], far[0], far[1]]
    offsets = [0 * gx, swap, step, step + swap, -step, -step + swap]
    lane = lax.broadcasted_iota(jnp.int32, (TILE, LANES), 1)
    for k in range(4):
        for half in range(2):
            block = jnp.zeros((TILE, LANES), F32)
            for n in range(4 * half, min(4 * half + 4, 6)):
                at = TILE * (n % 4)
                here = (lane >= at) & (lane < at + TILE)
                block = jnp.where(here, shifted(tiles[n], at - TILE * k), block)
            grid[pl.ds(TILE * k, TILE), pl.ds(LANES * half, LANES)] = block
    for n in range(6):
        start = pl.multiple_of((offsets[n] + 3) * TILE, TILE)
        cols[pl.ds(TILE * n, TILE), :] = col_ref[pl.ds(start, TILE), :]
    cols[pl.ds(6 * TILE, 2 * TILE), :] = jnp.zeros((2 * TILE, COLS), F32)
    across = jnp.dot(
        row_ref[gy], grid[...], precision=lax.Precision.HIGHEST, preferred_element_type=F32
    )
    smooth = jnp.dot(
        across, cols[...], precision=lax.Precision.HIGHEST, preferred_element_type=F32
    )
    factor = 1.0 - LOADING * smooth
    for i in range(TILE):
        rows = pl.ds(COARSEN * i, COARSEN)
        for t in range(2):
            piece = factor[i : i + 1, t * LANES : (t + 1) * LANES]
            out[rows, pl.ds(t * LANES, LANES)] = bare[t, rows, :] * piece


def run_etch(own, mate, near, far, bare):
    return pl.pallas_call(
        etch,
        in_specs=[VM] * 7,
        out_specs=VM,
        out_shape=jax.ShapeDtypeStruct((ROWS, COLS), F32),
        scratch_shapes=[pltpu.VMEM((4 * TILE, COLS), F32), pltpu.VMEM((COLS, COLS), F32)],
        compiler_params=params(4),
        name="etch",
    )(own, mate, near, far, bare, jnp.asarray(row_table()), jnp.asarray(column_table()))


def swap(block, axis, partner):
    count = lax.axis_size(axis)
    route = [(i, partner(i)) for i in range(count) if 0 <= partner(i) < count]
    return lax.ppermute(block, axis, route)


def inside(i):
    return i ^ 1


def outside(i):
    return i - 1 if i % 2 == 0 else i + 1


def shards(acid_field, quencher_field):
    acid_field = pltpu.with_memory_space_constraint(acid_field, pltpu.HBM)
    quencher_field = pltpu.with_memory_space_constraint(quencher_field, pltpu.HBM)
    first, second = pack_rows(acid_field, quencher_field)
    second = swap(second, "gy", outside)
    first = swap(first, "gy", inside)
    state = load_state(acid_field, quencher_field)
    state, first, second = pack_columns(state, first, second)
    second = swap(second, "gx", outside)
    first = swap(first, "gx", inside)
    state, edge, guard, density = run_bake(state, first, second)
    acid_after, inhibitor, bare = run_last(state, edge, guard)
    tile = density[:, :TILE]
    tile = jnp.concatenate([tile, swap(tile, "gy", lambda i: i ^ 1)], 1)
    own = jnp.concatenate([tile, swap(tile, "gy", lambda i: i ^ 2)], 1)
    mate = swap(own, "gx", inside)
    pair = jnp.stack([own, mate], 0)
    far = swap(pair, "gx", lambda i: i - 2 if i // 2 % 2 == 0 else i + 2)
    near = swap(pair, "gx", lambda i: i ^ 2)
    etch_rate = run_etch(own, mate, near, far, bare)
    return acid_after, inhibitor, etch_rate


def solution(mesh):
    in_specs = (P(None, "gy", "gx"), P(None, "gy", "gx"))
    out_specs = (P(None, "gy", "gx"), P(None, "gy", "gx"), P("gy", "gx"))
    return jax.shard_map(shards, mesh=mesh, in_specs=in_specs, out_specs=out_specs, check_vma=False)
```

```python
import jax
import jax.numpy as jnp
import numpy as np
from jax import lax
from jax.experimental import pallas as pl
from jax.experimental.pallas import tpu as pltpu
from jax.sharding import PartitionSpec as P

RATE_ACID = 0.15
RATE_QUENCH = 0.05
NEUTRAL = 0.1
DEPROTECT = 0.35
LOADING = 0.8
STEPS = 4
COARSEN = 8
REACH = 64
SPREAD = 25.0

LAYERS = 8
ROWS = 256
COLS = 256
LANES = 128
SUBS = 8
RUN = ROWS // SUBS
HALO = STEPS
BASE = 2 * SUBS
EXT = ROWS + 2 * BASE
LIVE = ROWS + BASE
FOLD = LIVE // SUBS // 2
PARTS = 4
TILE = ROWS // COARSEN
GROUP = 16

VM = pl.BlockSpec(memory_space=pltpu.VMEM)
HB = pl.BlockSpec(memory_space=pltpu.HBM)
F32 = jnp.float32


def params(mib):
    return pltpu.CompilerParams(vmem_limit_bytes=mib * 1024 * 1024)


def vmem(shape):
    return pltpu.VMEM(shape, F32)


def iota(dim):
    return lax.broadcasted_iota(jnp.int32, (SUBS, LANES), dim)


def row_strips(a_top, a_bot, q_top, q_bot, first_ref, second_ref):
    even = lax.rem(lax.axis_index("gy"), 2) == 0
    low = lax.broadcasted_iota(jnp.int32, (SUBS, COLS), 0) < HALO
    for d in range(LAYERS):
        top = jnp.where(low, a_top[d], pltpu.roll(q_top[d], HALO, 0))
        bot = jnp.where(low, pltpu.roll(a_bot[d], HALO, 0), q_bot[d])
        first_ref[d] = jnp.where(even, bot, top)
        second_ref[d] = jnp.where(even, top, bot)


def pack_rows(acid, quench):
    block = (LAYERS, SUBS, COLS)
    top = pl.BlockSpec(block, lambda i: (0, 0, 0))
    bot = pl.BlockSpec(block, lambda i: (0, RUN - 1, 0))
    out = jax.ShapeDtypeStruct(block, F32)
    return pl.pallas_call(
        row_strips,
        grid=(1,),
        in_specs=[top, bot, top, bot],
        out_specs=[pl.BlockSpec(block, lambda i: (0, 0, 0))] * 2,
        out_shape=[out, out],
        compiler_params=params(4),
        name="pack_rows",
    )(acid, acid, quench, quench)


def shifted(x, by):
    return pltpu.roll(x, by % LANES, 1)


def rows_at(i):
    return pl.ds(pl.multiple_of(i * SUBS, SUBS), SUBS)


def own_strips(state, strips, i):
    lane = iota(1)
    rows = rows_at(i)
    for f in range(2):
        left = jnp.zeros((SUBS, LANES), F32)
        right = jnp.zeros((SUBS, LANES), F32)
        for d in range(LAYERS):
            both = jnp.where(lane < LANES // 2, state[2 * f, d, rows, :], state[2 * f + 1, d, rows, :])
            moved = shifted(both, GROUP * d + HALO)
            at = lane - (GROUP * d + HALO)
            left = jnp.where((at >= 0) & (at < 8), moved, left)
            at = (lane + HALO) % LANES - GROUP * d
            right = jnp.where((at >= 0) & (at < 8), moved, right)
        strips[2 * f, rows, :] = left
        strips[2 * f + 1, rows, :] = right


def fill_state(acid, quench, state, strips, sems):
    size = ROWS // PARTS
    copies = []
    for p in range(PARTS):
        for t in range(4):
            source = (acid, quench)[t // 2].at[
                :, pl.ds(size * p, size), pl.ds((t % 2) * LANES, LANES)
            ]
            target = state.at[t, :, pl.ds(BASE + size * p, size), :]
            copy = pltpu.make_async_copy(source, target, sems.at[p, t])
            copy.start()
            copies.append(copy)
    for p in range(PARTS):
        for t in range(4):
            copies[4 * p + t].wait()

        def body(i, _):
            own_strips(state, strips, i)
            return 0

        first = (BASE + size * p) // SUBS
        lax.fori_loop(first, first + size // SUBS, body, 0)


def load_state(acid, quench):
    return pl.pallas_call(
        fill_state,
        in_specs=[HB, HB],
        out_specs=[VM, VM],
        out_shape=[vmem((4, LAYERS, EXT, LANES)), vmem((4, EXT, LANES))],
        scratch_shapes=[pltpu.SemaphoreType.DMA((PARTS, 4))],
        compiler_params=params(4),
        name="load_state",
    )(acid, quench)


def column_strips(state_in, strips_in, first_in, second_in, state, strips, first_ref, second_ref):
    del state_in, strips_in
    even_row = lax.rem(lax.axis_index("gy"), 2) == 0
    even_col = lax.rem(lax.axis_index("gx"), 2) == 0
    sub = iota(0)
    place = iota(1) % GROUP
    for d in range(LAYERS):
        for t in range(2):
            cols = pl.ds(t * LANES, LANES)
            one, two = first_in[d, :, cols], second_in[d, :, cols]
            top = jnp.where(even_row, two, one)
            bot = jnp.where(even_row, one, two)
            above, below = pl.ds(SUBS, SUBS), pl.ds(BASE + ROWS, SUBS)
            state[t, d, above, :] = jnp.where(sub >= HALO, pltpu.roll(top, HALO, 0), 0.0)
            state[2 + t, d, above, :] = jnp.where(sub >= HALO, top, 0.0)
            state[t, d, below, :] = jnp.where(sub < HALO, bot, 0.0)
            state[2 + t, d, below, :] = jnp.where(sub < HALO, pltpu.roll(bot, HALO, 0), 0.0)
    own_strips(state, strips, 1)
    own_strips(state, strips, (BASE + ROWS) // SUBS)
    for j in range(FOLD):
        left = jnp.zeros((SUBS, LANES), F32)
        right = jnp.zeros((SUBS, LANES), F32)
        for m in range(4):
            rows = pl.ds(SUBS * (1 + j + FOLD * (m // 2)), SUBS)
            at = (place - HALO - 4 * m) % GROUP
            left = jnp.where(at < HALO, shifted(strips[2 * (m % 2), rows, :], 4 * m), left)
            at = (place - 4 * m) % GROUP
            right = jnp.where(at < HALO, shifted(strips[2 * (m % 2) + 1, rows, :], 4 * m), right)
        first_ref[j] = jnp.where(even_col, right, left)
        second_ref[j] = jnp.where(even_col, left, right)


def pack_columns(state, strips, first, second):
    strip = jax.ShapeDtypeStruct((FOLD, SUBS, LANES), F32)
    return pl.pallas_call(
        column_strips,
        in_specs=[VM] * 4,
        out_specs=[VM] * 4,
        out_shape=[vmem((4, LAYERS, EXT, LANES)), vmem((4, EXT, LANES)), strip, strip],
        input_output_aliases={0: 0, 1: 1},
        compiler_params=params(4),
        name="pack_columns",
    )(state, strips, first, second)


def halves(x):
    high = x.astype(jnp.bfloat16)
    return high, (x - high.astype(F32)).astype(jnp.bfloat16)


def neighbour_sums(parts, matrix):
    split = [halves(x) for x in parts]
    stacked = jnp.concatenate([h for h, _ in split] + [l for _, l in split], 1)
    return jnp.dot(stacked, matrix, preferred_element_type=F32)


def beside_matrix():
    shape = (2 * COLS, COLS)
    row = lax.broadcasted_iota(jnp.int32, shape, 0) % COLS
    col = lax.broadcasted_iota(jnp.int32, shape, 1)
    return (jnp.abs(row - col) == 1).astype(jnp.bfloat16)


def strip_matrix(offset):
    shape = (2 * LANES, LANES)
    row = lax.broadcasted_iota(jnp.int32, shape, 0) % LANES
    col = lax.broadcasted_iota(jnp.int32, shape, 1)
    layer = ((col + offset) % LANES) // GROUP
    gap = (row - col + LANES) % LANES
    beside = ((gap == 1) | (gap == LANES - 1)).astype(F32)
    lower = (gap == jnp.where(layer == 0, 0, LANES - GROUP)).astype(F32)
    upper = (gap == jnp.where(layer == LAYERS - 1, 0, GROUP)).astype(F32)
    return (beside + lower + upper).astype(jnp.bfloat16)


def row_open(kind):
    gy = lax.axis_index("gy")
    if kind == 1:
        return 1.0
    outside = gy == 0 if kind == 0 else gy == lax.axis_size("gy") - 1
    return 1.0 - outside.astype(jnp.int32).astype(F32)


def sweep(body):
    for kind, low, high in ((0, 1, 2), (1, 2, 2 + RUN), (2, 2 + RUN, 3 + RUN)):

        def step(i, _, kind=kind):
            body(i, kind)
            return 0

        lax.fori_loop(low, high, step, 0)


def main_sums(src, sums, matrix, fields, start, count):
    for f in fields:
        parts = [src[2 * f + t, :, pl.ds(start, count), :].reshape(LAYERS * count, LANES) for t in range(2)]
        total = neighbour_sums(parts, matrix)
        for t in range(2):
            piece = total[:, t * LANES : (t + 1) * LANES].reshape(LAYERS, count, LANES)
            sums[2 * f + t, :, pl.ds(start, count), :] = piece


def main_steps(state, out, guard, one, two, sums, total, matrix):
    matrix[...] = beside_matrix()

    def advance(src, dst, visit):
        main_sums(src, sums, matrix[...], (0, 1), SUBS, LIVE)

        def body(i, kind):
            rows = rows_at(i)
            shut = row_open(kind)
            load = lambda d: [src[t, d, rows, :] for t in range(4)]
            before = center = load(0)
            for d in range(LAYERS):
                after = load(d + 1) if d + 1 < LAYERS else center
                around = []
                for t in range(4):
                    up = src[t, d, pl.ds(i * SUBS - 1, SUBS), :]
                    down = src[t, d, pl.ds(i * SUBS + 1, SUBS), :]
                    around.append((up + down) + (before[t] + after[t]) + sums[t, d, rows, :])
                for t in range(2):
                    scaled = NEUTRAL * center[t]
                    acid = RATE_ACID * around[t] + scaled * (1.0 - center[2 + t])
                    quench = RATE_QUENCH * around[2 + t] + center[2 + t] * (
                        (1.0 - 6.0 * RATE_QUENCH) - scaled
                    )
                    if kind != 1:
                        acid, quench = acid * shut, quench * shut
                    dst[t, d, rows, :] = acid
                    dst[2 + t, d, rows, :] = quench
                    if kind == 1:
                        visit(t, d, i, center[t], acid)
                before, center = center, after

        sweep(body)

    def begin(t, d, i, old, new):
        total[t, d, rows_at(i - 2), :] = old + new

    def protect(t, d, i, old, new):
        rows = rows_at(i - 2)
        guard[d, rows, pl.ds(t * LANES, LANES)] = jnp.exp(
            -DEPROTECT * (total[t, d, rows, :] + (old + new))
        )

    advance(state, one, begin)
    advance(one, two, lambda *_: None)
    advance(two, out, protect)


def run_main(state):
    grid = (4, LAYERS, EXT, LANES)
    return pl.pallas_call(
        main_steps,
        in_specs=[VM],
        out_specs=[VM, VM],
        out_shape=[vmem(grid), vmem((LAYERS, ROWS, COLS))],
        scratch_shapes=[
            pltpu.VMEM(grid, F32),
            pltpu.VMEM(grid, F32),
            pltpu.VMEM(grid, F32),
            pltpu.VMEM((2, LAYERS, ROWS, LANES), F32),
            pltpu.VMEM((2 * COLS, COLS), jnp.bfloat16),
        ],
        compiler_params=params(28),
        cost_estimate=pl.CostEstimate(flops=10**9, bytes_accessed=3 * 10**7, transcendentals=0),
        name="main_steps",
    )(state)


def strip_sums(src, sums, matrices, fields):
    rows = pl.ds(SUBS, LIVE)
    for side in range(2):
        stacked = jnp.concatenate([src[2 * f + side, rows, :] for f in fields], 0)
        total = neighbour_sums([stacked], matrices[side])
        for n, f in enumerate(fields):
            sums[2 * f + side, rows, :] = total[n * LIVE : (n + 1) * LIVE]


def strip_open():
    gx = lax.axis_index("gx")
    place = iota(1) % GROUP
    left = jnp.where((place < HALO) & (gx == 0), 0.0, 1.0)
    right = jnp.where((place >= HALO) & (place < 2 * HALO) & (gx == lax.axis_size("gx") - 1), 0.0, 1.0)
    return left, right


def put_edges(target, i, left, right, visit):
    lane = iota(1)
    rows = rows_at(i - 2)
    place = lane % GROUP
    both = jnp.where((place >= HALO) & (place < 2 * HALO), left, right)
    for d in range(LAYERS):
        moved = shifted(both, -GROUP * d - HALO)
        for t in range(2):
            here = lane < HALO if t == 0 else lane >= LANES - HALO
            cols = pl.ds(t * LANES, LANES)
            value = jnp.where(here, moved, target[d, rows, cols])
            target[d, rows, cols] = value
            visit(d, t, value)


def strip_steps(strips, first_in, second_in, guard_in, out, guard, density, one, two, sums, total, pooled):
    del guard_in
    even_col = lax.rem(lax.axis_index("gx"), 2) == 0
    place = iota(1) % GROUP
    opens = strip_open()
    matrices = strip_matrix(0), strip_matrix(HALO)
    for j in range(FOLD):
        a, b = first_in[j], second_in[j]
        left = jnp.where(even_col, b, a)
        right = jnp.where(even_col, a, b)
        for m in range(4):
            rows = pl.ds(SUBS * (1 + j + FOLD * (m // 2)), SUBS)
            f = m % 2
            one[2 * f, rows, :] = jnp.where(
                place < HALO, shifted(left, -4 * m), strips[2 * f, rows, :]
            )
            one[2 * f + 1, rows, :] = jnp.where(
                (place >= HALO) & (place < 2 * HALO),
                shifted(right, -4 * m),
                strips[2 * f + 1, rows, :],
            )

    def advance(src, dst, visit):
        strip_sums(src, sums, matrices, (0, 1))

        def body(i, kind):
            rows = rows_at(i)
            for side in range(2):
                shut = opens[side] * row_open(kind)
                center = [src[2 * f + side, rows, :] for f in range(2)]
                around = []
                for f in range(2):
                    up = src[2 * f + side, pl.ds(i * SUBS - 1, SUBS), :]
                    down = src[2 * f + side, pl.ds(i * SUBS + 1, SUBS), :]
                    around.append((up + down) + sums[2 * f + side, rows, :])
                scaled = NEUTRAL * center[0]
                acid = RATE_ACID * around[0] + scaled * (1.0 - center[1])
                quench = RATE_QUENCH * around[1] + center[1] * ((1.0 - 6.0 * RATE_QUENCH) - scaled)
                acid = acid * shut
                dst[side, rows, :] = acid
                dst[2 + side, rows, :] = quench * shut
                visit(side, rows, center[0], acid)

        sweep(body)

    def begin(side, rows, old, new):
        total[side, rows, :] = old + new

    def protect(side, rows, old, new):
        total[side, rows, :] = jnp.exp(-DEPROTECT * (total[side, rows, :] + (old + new)))

    advance(one, two, begin)
    advance(two, one, lambda *_: None)
    advance(one, out, protect)

    def merge(i, _):
        kept = [None, None]

        def add(d, t, value):
            kept[t] = value if d == 0 else kept[t] + value

        put_edges(guard, i, total[0, rows_at(i), :], total[1, rows_at(i), :], add)
        for t in range(2):
            pooled[rows_at(i - 2), pl.ds(t * LANES, LANES)] = kept[t]
        return 0

    lax.fori_loop(2, 2 + RUN, merge, 0)
    fine = pooled[...].reshape(TILE, COARSEN, COLS).sum(1)
    col = lax.broadcasted_iota(jnp.int32, (COLS, LANES), 0)
    block = lax.broadcasted_iota(jnp.int32, (COLS, LANES), 1)
    pool = (col // COARSEN == block).astype(F32)
    coarse = jnp.dot(fine, pool, precision=lax.Precision.HIGHEST, preferred_element_type=F32)
    wide = lax.broadcasted_iota(jnp.int32, (TILE, LANES), 1)
    mean = 1.0 - coarse * (1.0 / (LAYERS * COARSEN * COARSEN))
    density[...] = jnp.where(wide < TILE, mean, 0.0)


def run_strips(strips, first, second, guard):
    edge = (4, EXT, LANES)
    whole = (LAYERS, ROWS, COLS)
    return pl.pallas_call(
        strip_steps,
        in_specs=[VM] * 4,
        out_specs=[VM] * 3,
        out_shape=[vmem(edge), vmem(whole), jax.ShapeDtypeStruct((TILE, LANES), F32)],
        input_output_aliases={3: 1},
        scratch_shapes=[
            pltpu.VMEM(edge, F32),
            pltpu.VMEM(edge, F32),
            pltpu.VMEM(edge, F32),
            pltpu.VMEM((2, EXT, LANES), F32),
            pltpu.VMEM((ROWS, COLS), F32),
        ],
        compiler_params=params(8),
        name="strip_steps",
    )(strips, first, second, guard)


def last_step(state, strips, acid_out, sums, edge_sums, matrix, land, sems):
    matrix[...] = beside_matrix()
    main_sums(state, sums, matrix[...], (0,), BASE, ROWS)
    strip_sums(strips, edge_sums, (strip_matrix(0), strip_matrix(HALO)), (0,))

    def body(i, _):
        rows = rows_at(i)
        up_rows, down_rows = pl.ds(i * SUBS - 1, SUBS), pl.ds(i * SUBS + 1, SUBS)
        for t in range(2):
            before = center = state[t, 0, rows, :]
            for d in range(LAYERS):
                after = state[t, d + 1, rows, :] if d + 1 < LAYERS else center
                around = (state[t, d, up_rows, :] + state[t, d, down_rows, :]) + (
                    before + after
                ) + sums[t, d, rows, :]
                land[d, rows_at(i - 2), pl.ds(t * LANES, LANES)] = RATE_ACID * around + (
                    NEUTRAL * center
                ) * (1.0 - state[2 + t, d, rows, :])
                before, center = center, after
        edges = []
        for side in range(2):
            center = strips[side, rows, :]
            around = (strips[side, up_rows, :] + strips[side, down_rows, :]) + edge_sums[side, rows, :]
            edges.append(RATE_ACID * around + (NEUTRAL * center) * (1.0 - strips[2 + side, rows, :]))
        put_edges(land, i, *edges, lambda *_: None)
        return 0

    size = ROWS // PARTS
    copies = []
    for p in range(PARTS):
        first = (BASE + size * p) // SUBS
        lax.fori_loop(first, first + size // SUBS, body, 0)
        part = pl.ds(size * p, size)
        copies.append(pltpu.make_async_copy(land.at[:, part, :], acid_out.at[:, part, :], sems.at[p]))
        copies[p].start()
    for copy in copies:
        copy.wait()


def run_last(state, strips):
    whole = (LAYERS, ROWS, COLS)
    return pl.pallas_call(
        last_step,
        in_specs=[VM] * 2,
        out_specs=HB,
        out_shape=jax.ShapeDtypeStruct(whole, F32),
        scratch_shapes=[
            pltpu.VMEM((2, LAYERS, EXT, LANES), F32),
            pltpu.VMEM((2, EXT, LANES), F32),
            pltpu.VMEM((2 * COLS, COLS), jnp.bfloat16),
            pltpu.VMEM(whole, F32),
            pltpu.SemaphoreType.DMA((PARTS,)),
        ],
        compiler_params=params(12),
        name="last_step",
    )(state, strips)


def weights(distance):
    offset = np.arange(-REACH, REACH + 1, dtype=np.float64)
    norm = np.exp(-offset * offset / (2.0 * SPREAD * SPREAD)).sum()
    value = np.exp(-(distance.astype(np.float64) ** 2) / (2.0 * SPREAD * SPREAD))
    return np.where(np.abs(distance) <= REACH, value / norm, 0.0).astype(np.float32)


def row_table():
    p = np.arange(TILE)
    me = np.arange(4)[:, None, None, None]
    k = np.arange(4)[None, None, :, None]
    i = np.arange(TILE)[None, :, None, None]
    distance = TILE * ((me ^ k) - me) + p[None, None, None, :] - i
    return weights(distance).reshape(4, TILE, 4 * TILE)


def column_table():
    c = np.arange(7 * TILE)[:, None] - 3 * TILE
    return weights(c - np.arange(COLS)[None, :] // COARSEN)


def etch(own, mate, near, far, guard, row_ref, col_ref, out, grid, cols):
    gx, gy = lax.axis_index("gx"), lax.axis_index("gy")
    odd = lax.rem(gx, 2)
    upper = lax.rem(lax.div(gx, 2), 2)
    swap = 1 - 2 * odd
    step = 2 - 4 * upper
    tiles = [own[...], mate[...], near[0], near[1], far[0], far[1]]
    offsets = [0 * gx, swap, step, step + swap, -step, -step + swap]
    lane = lax.broadcasted_iota(jnp.int32, (TILE, LANES), 1)
    for k in range(4):
        for half in range(2):
            block = jnp.zeros((TILE, LANES), F32)
            for n in range(4 * half, min(4 * half + 4, 6)):
                at = TILE * (n % 4)
                here = (lane >= at) & (lane < at + TILE)
                block = jnp.where(here, shifted(tiles[n], at - TILE * k), block)
            grid[pl.ds(TILE * k, TILE), pl.ds(LANES * half, LANES)] = block
    for n in range(6):
        start = pl.multiple_of((offsets[n] + 3) * TILE, TILE)
        cols[pl.ds(TILE * n, TILE), :] = col_ref[pl.ds(start, TILE), :]
    cols[pl.ds(6 * TILE, 2 * TILE), :] = jnp.zeros((2 * TILE, COLS), F32)
    across = jnp.dot(
        row_ref[gy], grid[...], precision=lax.Precision.HIGHEST, preferred_element_type=F32
    )
    smooth = jnp.dot(
        across, cols[...], precision=lax.Precision.HIGHEST, preferred_element_type=F32
    )
    factor = 1.0 - LOADING * smooth
    for i in range(TILE):
        rows = pl.ds(COARSEN * i, COARSEN)
        for t in range(2):
            piece = factor[i : i + 1, t * LANES : (t + 1) * LANES]
            cols_of = pl.ds(t * LANES, LANES)
            out[rows, cols_of] = (1.0 - guard[0, rows, cols_of]) * piece


def run_etch(own, mate, near, far, guard):
    return pl.pallas_call(
        etch,
        in_specs=[VM] * 7,
        out_specs=VM,
        out_shape=jax.ShapeDtypeStruct((ROWS, COLS), F32),
        scratch_shapes=[pltpu.VMEM((4 * TILE, COLS), F32), pltpu.VMEM((COLS, COLS), F32)],
        compiler_params=params(4),
        name="etch",
    )(own, mate, near, far, guard, jnp.asarray(row_table()), jnp.asarray(column_table()))


def swap(block, axis, partner):
    count = lax.axis_size(axis)
    route = [(i, partner(i)) for i in range(count) if 0 <= partner(i) < count]
    return lax.ppermute(block, axis, route)


def inside(i):
    return i ^ 1


def outside(i):
    return i - 1 if i % 2 == 0 else i + 1


def shards(acid_field, quencher_field):
    acid_field = pltpu.with_memory_space_constraint(acid_field, pltpu.HBM)
    quencher_field = pltpu.with_memory_space_constraint(quencher_field, pltpu.HBM)
    first, second = pack_rows(acid_field, quencher_field)
    second = swap(second, "gy", outside)
    first = swap(first, "gy", inside)
    state, strips = load_state(acid_field, quencher_field)
    state, strips, first, second = pack_columns(state, strips, first, second)
    second = swap(second, "gx", outside)
    first = swap(first, "gx", inside)
    state, guard = run_main(state)
    strips, guard, density = run_strips(strips, first, second, guard)
    acid_after = run_last(state, strips)
    tile = density[:, :TILE]
    tile = jnp.concatenate([tile, swap(tile, "gy", lambda i: i ^ 1)], 1)
    own = jnp.concatenate([tile, swap(tile, "gy", lambda i: i ^ 2)], 1)
    mate = swap(own, "gx", inside)
    pair = jnp.stack([own, mate], 0)
    far = swap(pair, "gx", lambda i: i - 2 if i // 2 % 2 == 0 else i + 2)
    near = swap(pair, "gx", lambda i: i ^ 2)
    etch_rate = run_etch(own, mate, near, far, guard)
    return acid_after, guard, etch_rate


def solution(mesh):
    in_specs = (P(None, "gy", "gx"), P(None, "gy", "gx"))
    out_specs = (P(None, "gy", "gx"), P(None, "gy", "gx"), P("gy", "gx"))
    return jax.shard_map(shards, mesh=mesh, in_specs=in_specs, out_specs=out_specs, check_vma=False)
```

```python
import functools

import jax
import jax.numpy as jnp
import numpy as np
from jax import lax
from jax.experimental import pallas as pl
from jax.experimental.pallas import tpu as pltpu
from jax.sharding import PartitionSpec as P

RATE_ACID = 0.15
RATE_QUENCH = 0.05
NEUTRAL = 0.1
DEPROTECT = 0.35
LOADING = 0.8
STEPS = 4
COARSEN = 8
REACH = 64
SPREAD = 25.0

LAYERS = 8
ROWS = 256
COLS = 256
LANES = 128
SUBS = 8
RUN = ROWS // SUBS
HALO = STEPS
BASE = 2 * SUBS
EXT = ROWS + 2 * BASE
LIVE = ROWS + BASE
FOLD = LIVE // SUBS // 2
PARTS = 4
TILE = ROWS // COARSEN
BATCH = 4
GROUP = 16

VM = pl.BlockSpec(memory_space=pltpu.VMEM)
HB = pl.BlockSpec(memory_space=pltpu.HBM)
F32 = jnp.float32


def params(mib):
    return pltpu.CompilerParams(vmem_limit_bytes=mib * 1024 * 1024)


def vmem(shape):
    return pltpu.VMEM(shape, F32)


def iota(dim):
    return lax.broadcasted_iota(jnp.int32, (SUBS, LANES), dim)


def row_strips(a_top, a_bot, q_top, q_bot, first_ref, second_ref):
    even = lax.rem(lax.axis_index("gy"), 2) == 0
    low = lax.broadcasted_iota(jnp.int32, (SUBS, COLS), 0) < HALO
    for d in range(LAYERS):
        top = jnp.where(low, a_top[d], pltpu.roll(q_top[d], HALO, 0))
        bot = jnp.where(low, pltpu.roll(a_bot[d], HALO, 0), q_bot[d])
        first_ref[d] = jnp.where(even, bot, top)
        second_ref[d] = jnp.where(even, top, bot)


def pack_rows(acid, quench):
    block = (LAYERS, SUBS, COLS)
    top = pl.BlockSpec(block, lambda i: (0, 0, 0))
    bot = pl.BlockSpec(block, lambda i: (0, RUN - 1, 0))
    out = jax.ShapeDtypeStruct(block, F32)
    return pl.pallas_call(
        row_strips,
        grid=(1,),
        in_specs=[top, bot, top, bot],
        out_specs=[pl.BlockSpec(block, lambda i: (0, 0, 0))] * 2,
        out_shape=[out, out],
        compiler_params=params(4),
        name="pack_rows",
    )(acid, acid, quench, quench)


def shifted(x, by):
    return pltpu.roll(x, by % LANES, 1)


def rows_at(i):
    return pl.ds(pl.multiple_of(i * SUBS, SUBS), SUBS)


def own_edges(state, edges, i):
    lane = iota(1)
    rows = rows_at(i)
    for f in range(2):
        total = None
        for d in range(LAYERS):
            first = jnp.where(lane < 2 * HALO, state[2 * f, d, rows, :], 0.0)
            both = jnp.where(lane >= LANES - 2 * HALO, state[2 * f + 1, d, rows, :], first)
            moved = shifted(both, GROUP * d + HALO)
            total = moved if d == 0 else total + moved
        edges[f, rows, :] = total


def fill_state(acid, quench, state, edges, sems):
    size = ROWS // PARTS
    copies = []
    for p in range(PARTS):
        for t in range(4):
            source = (acid, quench)[t // 2].at[
                :, pl.ds(size * p, size), pl.ds((t % 2) * LANES, LANES)
            ]
            target = state.at[t, :, pl.ds(BASE + size * p, size), :]
            copy = pltpu.make_async_copy(source, target, sems.at[p, t])
            copy.start()
            copies.append(copy)
    for p in range(PARTS):
        for t in range(4):
            copies[4 * p + t].wait()

        def body(i, _):
            own_edges(state, edges, i)
            return 0

        first = (BASE + size * p) // SUBS
        lax.fori_loop(first, first + size // SUBS, body, 0, unroll=2)


def load_state(acid, quench):
    return pl.pallas_call(
        fill_state,
        in_specs=[HB, HB],
        out_specs=[VM, VM],
        out_shape=[vmem((4, LAYERS, EXT, LANES)), vmem((2, EXT, LANES))],
        scratch_shapes=[pltpu.SemaphoreType.DMA((PARTS, 4))],
        compiler_params=params(4),
        name="load_state",
    )(acid, quench)


def column_strips(state_in, edges_in, second_in, first_in, state, edges, second_ref, first_ref):
    del state_in, edges_in
    even_row = lax.rem(lax.axis_index("gy"), 2) == 0
    even_col = lax.rem(lax.axis_index("gx"), 2) == 0
    sub = iota(0)
    place = iota(1) % GROUP
    for d in range(LAYERS):
        for t in range(2):
            cols = pl.ds(t * LANES, LANES)
            one, two = first_in[d, :, cols], second_in[d, :, cols]
            top = jnp.where(even_row, two, one)
            bot = jnp.where(even_row, one, two)
            above, below = pl.ds(SUBS, SUBS), pl.ds(BASE + ROWS, SUBS)
            state[t, d, above, :] = jnp.where(sub >= HALO, pltpu.roll(top, HALO, 0), 0.0)
            state[2 + t, d, above, :] = jnp.where(sub >= HALO, top, 0.0)
            state[t, d, below, :] = jnp.where(sub < HALO, bot, 0.0)
            state[2 + t, d, below, :] = jnp.where(sub < HALO, pltpu.roll(bot, HALO, 0), 0.0)
    own_edges(state, edges, 1)
    own_edges(state, edges, (BASE + ROWS) // SUBS)
    for j in range(FOLD):
        left = jnp.zeros((SUBS, LANES), F32)
        right = jnp.zeros((SUBS, LANES), F32)
        for m in range(4):
            rows = pl.ds(SUBS * (1 + j + FOLD * (m // 2)), SUBS)
            moved = shifted(edges[m % 2, rows, :], 4 * m)
            left = jnp.where((place - HALO - 4 * m) % GROUP < HALO, moved, left)
            right = jnp.where((place - 4 * m) % GROUP < HALO, moved, right)
        first_ref[j] = jnp.where(even_col, right, left)
        second_ref[j] = jnp.where(even_col, left, right)


def pack_columns(state, edges, second, first):
    strip = jax.ShapeDtypeStruct((FOLD, SUBS, LANES), F32)
    return pl.pallas_call(
        column_strips,
        in_specs=[VM] * 4,
        out_specs=[VM] * 4,
        out_shape=[vmem((4, LAYERS, EXT, LANES)), vmem((2, EXT, LANES)), strip, strip],
        input_output_aliases={0: 0, 1: 1},
        compiler_params=params(4),
        name="pack_columns",
    )(state, edges, second, first)


def halves(x):
    high = x.astype(jnp.bfloat16)
    return high, (x - high.astype(F32)).astype(jnp.bfloat16)


def neighbour_sums(parts, matrix):
    split = [halves(x) for x in parts]
    stacked = jnp.concatenate([h for h, _ in split] + [l for _, l in split], 1)
    return jnp.dot(stacked, matrix, preferred_element_type=F32)


def beside_matrix():
    shape = (2 * COLS, COLS)
    row = lax.broadcasted_iota(jnp.int32, shape, 0) % COLS
    col = lax.broadcasted_iota(jnp.int32, shape, 1)
    return (jnp.abs(row - col) == 1).astype(jnp.bfloat16)


def strip_matrix(offset):
    shape = (2 * LANES, LANES)
    row = lax.broadcasted_iota(jnp.int32, shape, 0) % LANES
    col = lax.broadcasted_iota(jnp.int32, shape, 1)
    layer = ((col + offset) % LANES) // GROUP
    gap = (row - col + LANES) % LANES
    beside = ((gap == 1) | (gap == LANES - 1)).astype(F32)
    lower = (gap == jnp.where(layer == 0, 0, LANES - GROUP)).astype(F32)
    upper = (gap == jnp.where(layer == LAYERS - 1, 0, GROUP)).astype(F32)
    return (beside + lower + upper).astype(jnp.bfloat16)


def row_open(kind):
    gy = lax.axis_index("gy")
    if kind == 1:
        return 1.0
    outside = gy == 0 if kind == 0 else gy == lax.axis_size("gy") - 1
    return 1.0 - outside.astype(jnp.int32).astype(F32)


def sweep(body):
    def step(p, _):
        body(2 + p * BATCH, BATCH, 1)
        return 0

    body(1, 1, 0)
    lax.fori_loop(0, RUN // BATCH, step, 0)
    body(2 + RUN, 1, 2)


def beside_rows(read, center, i, mixed):
    n = len(center)
    above = [read(pl.ds((i + j) * SUBS - 1, SUBS)) for j in range(n)]
    if not mixed:
        return [above[j] + read(pl.ds((i + j) * SUBS + 1, SUBS)) for j in range(n)]
    last = iota(0) == SUBS - 1
    up = [pltpu.roll(x, SUBS - 1, 0) for x in center + [read(rows_at(i + n))]]
    return [above[j] + jnp.where(last, up[j + 1], up[j]) for j in range(n)]


def main_sums(src, sums, matrix, fields, start, count):
    for f in fields:
        parts = [src[2 * f + t, :, pl.ds(start, count), :].reshape(LAYERS * count, LANES) for t in range(2)]
        total = neighbour_sums(parts, matrix)
        for t in range(2):
            piece = total[:, t * LANES : (t + 1) * LANES].reshape(LAYERS, count, LANES)
            sums[2 * f + t, :, pl.ds(start, count), :] = piece


def main_steps(role, state, *refs):
    out, guard, one, two, sums, total, matrix = refs[-7:]

    @pl.when(lax.rem(lax.axis_index("gx"), 2) == role)
    def _():
        main_part(state, out, guard, one, two, sums, total, matrix)


def main_part(state, out, guard, one, two, sums, total, matrix):
    matrix[...] = beside_matrix()

    def advance(src, dst, visit):
        main_sums(src, sums, matrix[...], (0, 1), SUBS, LIVE)

        def body(i, n, kind):
            shut = row_open(kind)
            load = lambda d: [[src[t, d, rows_at(i + j), :] for j in range(n)] for t in range(4)]
            before = center = load(0)
            for d in range(LAYERS):
                after = load(d + 1) if d + 1 < LAYERS else center
                around = []
                for t in range(4):
                    rows = beside_rows(lambda r, t=t, d=d: src[t, d, r, :], center[t], i, t % 2 == 1)
                    around.append(
                        [
                            (rows[j] + (before[t][j] + after[t][j])) + sums[t, d, rows_at(i + j), :]
                            for j in range(n)
                        ]
                    )
                for t in range(2):
                    for j in range(n):
                        at = rows_at(i + j)
                        scaled = NEUTRAL * center[t][j]
                        acid = RATE_ACID * around[t][j] + scaled * (1.0 - center[2 + t][j])
                        quench = RATE_QUENCH * around[2 + t][j] + center[2 + t][j] * (
                            (1.0 - 6.0 * RATE_QUENCH) - scaled
                        )
                        if kind != 1:
                            acid, quench = acid * shut, quench * shut
                        dst[t, d, at, :] = acid
                        dst[2 + t, d, at, :] = quench
                        if kind == 1:
                            visit(t, d, i + j, center[t][j], acid)
                before, center = center, after

        sweep(body)

    def begin(t, d, i, old, new):
        total[t, d, rows_at(i - 2), :] = old + new

    def protect(t, d, i, old, new):
        rows = rows_at(i - 2)
        guard[d, rows, pl.ds(t * LANES, LANES)] = jnp.exp(
            -DEPROTECT * (total[t, d, rows, :] + (old + new))
        )

    advance(state, one, begin)
    advance(one, two, lambda *_: None)
    advance(two, out, protect)


def run_main(role, state, *earlier):
    grid = (4, LAYERS, EXT, LANES)
    return pl.pallas_call(
        functools.partial(main_steps, role),
        in_specs=[VM] * (1 + len(earlier)),
        out_specs=[VM, VM],
        out_shape=[vmem(grid), vmem((LAYERS, ROWS, COLS))],
        input_output_aliases={1: 0, 2: 1} if earlier else {},
        scratch_shapes=[
            pltpu.VMEM(grid, F32),
            pltpu.VMEM(grid, F32),
            pltpu.VMEM(grid, F32),
            pltpu.VMEM((2, LAYERS, ROWS, LANES), F32),
            pltpu.VMEM((2 * COLS, COLS), jnp.bfloat16),
        ],
        compiler_params=params(28),
        cost_estimate=pl.CostEstimate(
            flops=(10**9, 1)[role], bytes_accessed=(3 * 10**7, 1)[role], transcendentals=0
        ),
        name=("main_even", "main_odd")[role],
    )(state, *earlier)


def strip_sums(src, sums, matrices, fields):
    rows = pl.ds(SUBS, LIVE)
    for side in range(2):
        stacked = jnp.concatenate([src[2 * f + side, rows, :] for f in fields], 0)
        total = neighbour_sums([stacked], matrices[side])
        for n, f in enumerate(fields):
            sums[2 * f + side, rows, :] = total[n * LIVE : (n + 1) * LIVE]


def strip_open():
    gx = lax.axis_index("gx")
    place = iota(1) % GROUP
    left = jnp.where((place < HALO) & (gx == 0), 0.0, 1.0)
    right = jnp.where((place >= HALO) & (place < 2 * HALO) & (gx == lax.axis_size("gx") - 1), 0.0, 1.0)
    return left, right


def put_edges(target, i, left, right, visit):
    lane = iota(1)
    rows = rows_at(i - 2)
    place = lane % GROUP
    both = jnp.where((place >= HALO) & (place < 2 * HALO), left, right)
    for d in range(LAYERS):
        moved = shifted(both, -GROUP * d - HALO)
        for t in range(2):
            here = lane < HALO if t == 0 else lane >= LANES - HALO
            cols = pl.ds(t * LANES, LANES)
            value = jnp.where(here, moved, target[d, rows, cols])
            target[d, rows, cols] = value
            visit(d, t, value)


def strip_steps(edges, inner_in, up_in, down_in, guard_in, out, guard, density, one, two, sums, total, pooled):
    del guard_in
    even_col = lax.rem(lax.axis_index("gx"), 2) == 0
    place = iota(1) % GROUP
    opens = strip_open()
    matrices = strip_matrix(0), strip_matrix(HALO)
    for j in range(FOLD):
        left = jnp.where(even_col, up_in[j], inner_in[j])
        right = jnp.where(even_col, inner_in[j], down_in[j])
        for m in range(4):
            rows = pl.ds(SUBS * (1 + j + FOLD * (m // 2)), SUBS)
            f = m % 2
            own = edges[f, rows, :]
            near = (place >= HALO) & (place < 2 * HALO)
            kept = jnp.where((place >= HALO) & (place < 3 * HALO), own, 0.0)
            one[2 * f, rows, :] = jnp.where(place < HALO, shifted(left, -4 * m), kept)
            kept = jnp.where((place < HALO) | (place >= 3 * HALO), own, 0.0)
            one[2 * f + 1, rows, :] = jnp.where(near, shifted(right, -4 * m), kept)

    def advance(src, dst, visit):
        strip_sums(src, sums, matrices, (0, 1))

        def body(i, n, kind):
            for side in range(2):
                shut = opens[side] * row_open(kind)
                for j in range(n):
                    rows = rows_at(i + j)
                    center = [src[2 * f + side, rows, :] for f in range(2)]
                    around = []
                    for f in range(2):
                        read = lambda r, f=f, side=side: src[2 * f + side, r, :]
                        beside = beside_rows(read, [center[f]], i + j, False)
                        around.append(beside[0] + sums[2 * f + side, rows, :])
                    scaled = NEUTRAL * center[0]
                    acid = RATE_ACID * around[0] + scaled * (1.0 - center[1])
                    quench = RATE_QUENCH * around[1] + center[1] * (
                        (1.0 - 6.0 * RATE_QUENCH) - scaled
                    )
                    acid = acid * shut
                    dst[side, rows, :] = acid
                    dst[2 + side, rows, :] = quench * shut
                    visit(side, rows, center[0], acid)

        sweep(body)

    def begin(side, rows, old, new):
        total[side, rows, :] = old + new

    def protect(side, rows, old, new):
        total[side, rows, :] = jnp.exp(-DEPROTECT * (total[side, rows, :] + (old + new)))

    advance(one, two, begin)
    advance(two, one, lambda *_: None)
    advance(one, out, protect)

    def merge(i, _):
        kept = [None, None]

        def add(d, t, value):
            kept[t] = value if d == 0 else kept[t] + value

        put_edges(guard, i, total[0, rows_at(i), :], total[1, rows_at(i), :], add)
        for t in range(2):
            pooled[rows_at(i - 2), pl.ds(t * LANES, LANES)] = kept[t]
        return 0

    lax.fori_loop(2, 2 + RUN, merge, 0, unroll=2)
    fine = pooled[...].reshape(TILE, COARSEN, COLS).sum(1)
    col = lax.broadcasted_iota(jnp.int32, (COLS, LANES), 0)
    block = lax.broadcasted_iota(jnp.int32, (COLS, LANES), 1)
    pool = (col // COARSEN == block).astype(F32)
    coarse = jnp.dot(fine, pool, precision=lax.Precision.HIGHEST, preferred_element_type=F32)
    wide = lax.broadcasted_iota(jnp.int32, (TILE, LANES), 1)
    mean = 1.0 - coarse * (1.0 / (LAYERS * COARSEN * COARSEN))
    density[...] = jnp.where(wide < TILE, mean, 0.0)


def run_strips(edges, inner, up, down, guard):
    edge = (4, EXT, LANES)
    whole = (LAYERS, ROWS, COLS)
    return pl.pallas_call(
        strip_steps,
        in_specs=[VM] * 5,
        out_specs=[VM] * 3,
        out_shape=[vmem(edge), vmem(whole), jax.ShapeDtypeStruct((TILE, LANES), F32)],
        input_output_aliases={4: 1},
        scratch_shapes=[
            pltpu.VMEM(edge, F32),
            pltpu.VMEM(edge, F32),
            pltpu.VMEM(edge, F32),
            pltpu.VMEM((2, EXT, LANES), F32),
            pltpu.VMEM((ROWS, COLS), F32),
        ],
        compiler_params=params(8),
        name="strip_steps",
    )(edges, inner, up, down, guard)


def last_step(
    state, strips, guard, col_ref, acid_out, guard_out, cols, sums, edge_sums, matrix, land, sems
):
    kept = pltpu.make_async_copy(guard, guard_out, sems.at[PARTS])
    kept.start()
    matrix[...] = beside_matrix()
    main_sums(state, sums, matrix[...], (0,), BASE, ROWS)
    strip_sums(strips, edge_sums, (strip_matrix(0), strip_matrix(HALO)), (0,))
    n = BATCH

    def body(p, _):
        i = 2 + p * n
        for t in range(2):
            load = lambda d, t=t: [state[t, d, rows_at(i + j), :] for j in range(n)]
            before = center = load(0)
            for d in range(LAYERS):
                after = load(d + 1) if d + 1 < LAYERS else center
                rows = beside_rows(lambda r, t=t, d=d: state[t, d, r, :], center, i, t == 1)
                for j in range(n):
                    at = rows_at(i + j)
                    around = (rows[j] + (before[j] + after[j])) + sums[t, d, at, :]
                    land[d, rows_at(i + j - 2), pl.ds(t * LANES, LANES)] = RATE_ACID * around + (
                        NEUTRAL * center[j]
                    ) * (1.0 - state[2 + t, d, at, :])
                before, center = center, after
        for j in range(n):
            at = rows_at(i + j)
            edges = []
            for side in range(2):
                center = strips[side, at, :]
                beside = beside_rows(lambda r, side=side: strips[side, r, :], [center], i + j, False)
                around = beside[0] + edge_sums[side, at, :]
                edges.append(
                    RATE_ACID * around + (NEUTRAL * center) * (1.0 - strips[2 + side, at, :])
                )
            put_edges(land, i + j, *edges, lambda *_: None)
        return 0

    size = ROWS // PARTS
    copies = []
    for p in range(PARTS):
        count = size // SUBS // n
        lax.fori_loop(p * count, (p + 1) * count, body, 0)
        part = pl.ds(size * p, size)
        copies.append(pltpu.make_async_copy(land.at[:, part, :], acid_out.at[:, part, :], sems.at[p]))
        copies[p].start()
    for m, offset in enumerate(tile_offsets()):
        start = pl.multiple_of((offset + 3) * TILE, TILE)
        cols[pl.ds(TILE * m, TILE), :] = col_ref[pl.ds(start, TILE), :]
    for copy in copies:
        copy.wait()
    kept.wait()


def run_last(state, strips, guard):
    whole = jax.ShapeDtypeStruct((LAYERS, ROWS, COLS), F32)
    return pl.pallas_call(
        last_step,
        in_specs=[VM] * 4,
        out_specs=[HB, HB, VM],
        out_shape=[whole, whole, vmem((6 * TILE, COLS))],
        scratch_shapes=[
            pltpu.VMEM((2, LAYERS, EXT, LANES), F32),
            pltpu.VMEM((2, EXT, LANES), F32),
            pltpu.VMEM((2 * COLS, COLS), jnp.bfloat16),
            pltpu.VMEM((LAYERS, ROWS, COLS), F32),
            pltpu.SemaphoreType.DMA((PARTS + 1,)),
        ],
        compiler_params=params(12),
        cost_estimate=pl.CostEstimate(flops=10**9, bytes_accessed=10**7, transcendentals=0),
        name="last_step",
    )(state, strips, guard, jnp.asarray(column_table()))


def weights(distance):
    offset = np.arange(-REACH, REACH + 1, dtype=np.float64)
    norm = np.exp(-offset * offset / (2.0 * SPREAD * SPREAD)).sum()
    value = np.exp(-(distance.astype(np.float64) ** 2) / (2.0 * SPREAD * SPREAD))
    return np.where(np.abs(distance) <= REACH, value / norm, 0.0).astype(np.float32)


def row_table():
    p = np.arange(TILE)
    me = np.arange(4)[:, None, None, None]
    k = np.arange(4)[None, None, :, None]
    i = np.arange(TILE)[None, :, None, None]
    distance = TILE * ((me ^ k) - me) + p[None, None, None, :] - i
    return weights(distance).reshape(4, TILE, 4 * TILE)


def column_table():
    c = np.arange(7 * TILE)[:, None] - 3 * TILE
    return weights(c - np.arange(COLS)[None, :] // COARSEN)


def tile_offsets():
    gx = lax.axis_index("gx")
    beside = 1 - 2 * lax.rem(gx, 2)
    step = 2 - 4 * lax.rem(lax.div(gx, 2), 2)
    return [0 * gx, beside, step, step + beside, -step, -step + beside]


def etch(low, high, guard, row_ref, cols, out):
    gy = lax.axis_index("gy")
    across = sum(
        jnp.dot(
            row_ref[gy, :, pl.ds(2 * TILE * n, 2 * TILE)],
            part[...],
            precision=lax.Precision.HIGHEST,
            preferred_element_type=F32,
        )
        for n, part in enumerate((low, high))
    )
    smooth = jnp.dot(across, cols[...], precision=lax.Precision.HIGHEST, preferred_element_type=F32)
    factor = 1.0 - LOADING * smooth
    for i in range(TILE):
        rows = pl.ds(COARSEN * i, COARSEN)
        for t in range(2):
            piece = factor[i : i + 1, t * LANES : (t + 1) * LANES]
            cols_of = pl.ds(t * LANES, LANES)
            out[rows, cols_of] = (1.0 - guard[0, rows, cols_of]) * piece


def run_etch(low, high, guard, cols):
    return pl.pallas_call(
        etch,
        in_specs=[VM] * 5,
        out_specs=VM,
        out_shape=jax.ShapeDtypeStruct((ROWS, COLS), F32),
        compiler_params=params(4),
        name="etch",
    )(low, high, guard, jnp.asarray(row_table()), cols)


def swap(block, axis, partner):
    count = lax.axis_size(axis)
    route = [(i, partner(i)) for i in range(count) if 0 <= partner(i) < count]
    return lax.ppermute(block, axis, route)


def shift(block, axis, odd):
    count = lax.axis_size(axis)
    route = [(i, i + 2 * odd - 1) for i in range(count) if i % 2 == odd]
    return lax.ppermute(block, axis, [(i, k) for i, k in route if 0 <= k < count])


def inside(i):
    return i ^ 1


def outside(i):
    return i - 1 if i % 2 == 0 else i + 1


def shards(acid_field, quencher_field):
    acid_field = pltpu.with_memory_space_constraint(acid_field, pltpu.HBM)
    quencher_field = pltpu.with_memory_space_constraint(quencher_field, pltpu.HBM)
    first, second = pack_rows(acid_field, quencher_field)
    second = swap(second, "gy", outside)
    first = swap(first, "gy", inside)
    state, edges = load_state(acid_field, quencher_field)
    state, edges, second, first = pack_columns(state, edges, second, first)
    inner = swap(first, "gx", inside)
    up = shift(second, "gx", 1)
    state_even, guard = run_main(0, state)
    second, state_even = lax.optimization_barrier((second, state_even))
    down = shift(second, "gx", 0)
    up, state_even = lax.optimization_barrier((up, state_even))
    state, guard = run_main(1, state, state_even, guard)
    strips, guard, density = run_strips(edges, inner, up, down, guard)
    tile = density[:, :TILE]
    pair = jnp.concatenate([tile, swap(tile, "gx", inside)], 1)
    far = swap(pair, "gx", lambda i: i - 2 if i // 2 % 2 == 0 else i + 2)
    near = swap(pair, "gx", lambda i: i ^ 2)
    acid_after, inhibitor, cols = run_last(state, strips, guard)
    near, far, cols = lax.optimization_barrier((near, far, cols))
    six = jnp.concatenate([pair, near, far], 1)
    low = jnp.concatenate([six, swap(six, "gy", lambda i: i ^ 1)], 0)
    high = swap(low, "gy", lambda i: i ^ 2)
    etch_rate = run_etch(low, high, guard, cols)
    return acid_after, inhibitor, etch_rate


def solution(mesh):
    in_specs = (P(None, "gy", "gx"), P(None, "gy", "gx"))
    out_specs = (P(None, "gy", "gx"), P(None, "gy", "gx"), P("gy", "gx"))
    return jax.shard_map(shards, mesh=mesh, in_specs=in_specs, out_specs=out_specs, check_vma=False)
```

```python
import functools

import jax
import jax.numpy as jnp
import numpy as np
from jax import lax
from jax.experimental import pallas as pl
from jax.experimental.pallas import tpu as pltpu
from jax.sharding import PartitionSpec as P

RATE_ACID = 0.15
RATE_QUENCH = 0.05
NEUTRAL = 0.1
DEPROTECT = 0.35
LOADING = 0.8
STEPS = 4
COARSEN = 8
REACH = 64
SPREAD = 25.0

LAYERS = 8
ROWS = 256
COLS = 256
LANES = 128
SUBS = 8
RUN = ROWS // SUBS
HALO = STEPS
BASE = 2 * SUBS
EXT = ROWS + 2 * BASE
LIVE = ROWS + BASE
FOLD = LIVE // SUBS // 2
PARTS = 4
TILE = ROWS // COARSEN
BATCH = 4
GROUP = 16

VM = pl.BlockSpec(memory_space=pltpu.VMEM)
HB = pl.BlockSpec(memory_space=pltpu.HBM)
F32 = jnp.float32


def params(mib):
    return pltpu.CompilerParams(vmem_limit_bytes=mib * 1024 * 1024)


EARLY_COLUMNS = (0, 1, 4, 6)
PERIOD = 8


def early_column(i):
    return sum((i % PERIOD == k) * 1 for k in EARLY_COLUMNS)


def is_early():
    place = lax.rem(lax.axis_index("gx"), PERIOD)
    return functools.reduce(jnp.logical_or, [place == k for k in EARLY_COLUMNS])


def vmem(shape):
    return pltpu.VMEM(shape, F32)


def iota(dim):
    return lax.broadcasted_iota(jnp.int32, (SUBS, LANES), dim)


def row_strips(a_top, a_bot, q_top, q_bot, first_ref, second_ref):
    even = lax.rem(lax.axis_index("gy"), 2) == 0
    low = lax.broadcasted_iota(jnp.int32, (SUBS, COLS), 0) < HALO
    for d in range(LAYERS):
        top = jnp.where(low, a_top[d], pltpu.roll(q_top[d], HALO, 0))
        bot = jnp.where(low, pltpu.roll(a_bot[d], HALO, 0), q_bot[d])
        first_ref[d] = jnp.where(even, bot, top)
        second_ref[d] = jnp.where(even, top, bot)


def pack_rows(acid, quench):
    block = (LAYERS, SUBS, COLS)
    top = pl.BlockSpec(block, lambda i: (0, 0, 0))
    bot = pl.BlockSpec(block, lambda i: (0, RUN - 1, 0))
    out = jax.ShapeDtypeStruct(block, F32)
    return pl.pallas_call(
        row_strips,
        grid=(1,),
        in_specs=[top, bot, top, bot],
        out_specs=[pl.BlockSpec(block, lambda i: (0, 0, 0))] * 2,
        out_shape=[out, out],
        compiler_params=params(4),
        name="pack_rows",
    )(acid, acid, quench, quench)


def shifted(x, by):
    return pltpu.roll(x, by % LANES, 1)


def rows_at(i):
    return pl.ds(pl.multiple_of(i * SUBS, SUBS), SUBS)


def own_edges(state, edges, i):
    lane = iota(1)
    rows = rows_at(i)
    for f in range(2):
        total = None
        for d in range(LAYERS):
            first = jnp.where(lane < 2 * HALO, state[2 * f, d, rows, :], 0.0)
            both = jnp.where(lane >= LANES - 2 * HALO, state[2 * f + 1, d, rows, :], first)
            moved = shifted(both, GROUP * d + HALO)
            total = moved if d == 0 else total + moved
        edges[f, rows, :] = total


def fill_state(acid, quench, state, edges, sems):
    size = ROWS // PARTS
    copies = []
    for p in range(PARTS):
        for t in range(4):
            source = (acid, quench)[t // 2].at[
                :, pl.ds(size * p, size), pl.ds((t % 2) * LANES, LANES)
            ]
            target = state.at[t, :, pl.ds(BASE + size * p, size), :]
            copy = pltpu.make_async_copy(source, target, sems.at[p, t])
            copy.start()
            copies.append(copy)
    for p in range(PARTS):
        for t in range(4):
            copies[4 * p + t].wait()

        def body(i, _):
            own_edges(state, edges, i)
            return 0

        first = (BASE + size * p) // SUBS
        lax.fori_loop(first, first + size // SUBS, body, 0, unroll=4)


def load_state(acid, quench):
    return pl.pallas_call(
        fill_state,
        in_specs=[HB, HB],
        out_specs=[VM, VM],
        out_shape=[vmem((4, LAYERS, EXT, LANES)), vmem((2, EXT, LANES))],
        scratch_shapes=[pltpu.SemaphoreType.DMA((PARTS, 4))],
        compiler_params=params(4),
        name="load_state",
    )(acid, quench)


def column_strips(state_in, edges_in, second_in, first_in, state, edges, second_ref, first_ref):
    del state_in, edges_in
    even_row = lax.rem(lax.axis_index("gy"), 2) == 0
    even_col = lax.rem(lax.axis_index("gx"), 2) == 0
    sub = iota(0)
    place = iota(1) % GROUP
    for d in range(LAYERS):
        for t in range(2):
            cols = pl.ds(t * LANES, LANES)
            one, two = first_in[d, :, cols], second_in[d, :, cols]
            top = jnp.where(even_row, two, one)
            bot = jnp.where(even_row, one, two)
            above, below = pl.ds(SUBS, SUBS), pl.ds(BASE + ROWS, SUBS)
            state[t, d, above, :] = jnp.where(sub >= HALO, pltpu.roll(top, HALO, 0), 0.0)
            state[2 + t, d, above, :] = jnp.where(sub >= HALO, top, 0.0)
            state[t, d, below, :] = jnp.where(sub < HALO, bot, 0.0)
            state[2 + t, d, below, :] = jnp.where(sub < HALO, pltpu.roll(bot, HALO, 0), 0.0)
    own_edges(state, edges, 1)
    own_edges(state, edges, (BASE + ROWS) // SUBS)
    for j in range(FOLD):
        left = jnp.zeros((SUBS, LANES), F32)
        right = jnp.zeros((SUBS, LANES), F32)
        for m in range(4):
            rows = pl.ds(SUBS * (1 + j + FOLD * (m // 2)), SUBS)
            moved = shifted(edges[m % 2, rows, :], 4 * m)
            left = jnp.where((place - HALO - 4 * m) % GROUP < HALO, moved, left)
            right = jnp.where((place - 4 * m) % GROUP < HALO, moved, right)
        first_ref[j] = jnp.where(even_col, right, left)
        second_ref[j] = jnp.where(even_col, left, right)


def pack_columns(state, edges, second, first):
    strip = jax.ShapeDtypeStruct((FOLD, SUBS, LANES), F32)
    return pl.pallas_call(
        column_strips,
        in_specs=[VM] * 4,
        out_specs=[VM] * 4,
        out_shape=[vmem((4, LAYERS, EXT, LANES)), vmem((2, EXT, LANES)), strip, strip],
        input_output_aliases={0: 0, 1: 1},
        compiler_params=params(4),
        name="pack_columns",
    )(state, edges, second, first)


def halves(x):
    high = x.astype(jnp.bfloat16)
    return high, (x - high.astype(F32)).astype(jnp.bfloat16)


def neighbour_sums(parts, matrix):
    split = [halves(x) for x in parts]
    stacked = jnp.concatenate([h for h, _ in split] + [l for _, l in split], 1)
    return jnp.dot(stacked, matrix, preferred_element_type=F32)


def beside_matrix():
    shape = (2 * COLS, COLS)
    row = lax.broadcasted_iota(jnp.int32, shape, 0) % COLS
    col = lax.broadcasted_iota(jnp.int32, shape, 1)
    return (jnp.abs(row - col) == 1).astype(jnp.bfloat16)


def strip_matrix(offset):
    shape = (2 * LANES, LANES)
    row = lax.broadcasted_iota(jnp.int32, shape, 0) % LANES
    col = lax.broadcasted_iota(jnp.int32, shape, 1)
    layer = ((col + offset) % LANES) // GROUP
    gap = (row - col + LANES) % LANES
    beside = ((gap == 1) | (gap == LANES - 1)).astype(F32)
    lower = (gap == jnp.where(layer == 0, 0, LANES - GROUP)).astype(F32)
    upper = (gap == jnp.where(layer == LAYERS - 1, 0, GROUP)).astype(F32)
    return (beside + lower + upper).astype(jnp.bfloat16)


def row_open(kind):
    gy = lax.axis_index("gy")
    if kind == 1:
        return 1.0
    outside = gy == 0 if kind == 0 else gy == lax.axis_size("gy") - 1
    return 1.0 - outside.astype(jnp.int32).astype(F32)


def sweep(body):
    def step(p, _):
        body(2 + p * BATCH, BATCH, 1)
        return 0

    body(1, 1, 0)
    lax.fori_loop(0, RUN // BATCH, step, 0)
    body(2 + RUN, 1, 2)


def beside_rows(read, center, i, mixed):
    n = len(center)
    above = [read(pl.ds((i + j) * SUBS - 1, SUBS)) for j in range(n)]
    if not mixed:
        return [above[j] + read(pl.ds((i + j) * SUBS + 1, SUBS)) for j in range(n)]
    last = iota(0) == SUBS - 1
    up = [pltpu.roll(x, SUBS - 1, 0) for x in center + [read(rows_at(i + n))]]
    return [above[j] + jnp.where(last, up[j + 1], up[j]) for j in range(n)]


def main_sums(src, sums, matrix, fields, start, count):
    for f in fields:
        parts = [src[2 * f + t, :, pl.ds(start, count), :].reshape(LAYERS * count, LANES) for t in range(2)]
        total = neighbour_sums(parts, matrix)
        for t in range(2):
            piece = total[:, t * LANES : (t + 1) * LANES].reshape(LAYERS, count, LANES)
            sums[2 * f + t, :, pl.ds(start, count), :] = piece


def main_steps(role, state, *refs):
    out, guard, one, two, sums, total, matrix = refs[-7:]

    @pl.when(is_early() == (role == 0))
    def _():
        main_part(state, out, guard, one, two, sums, total, matrix)


def main_part(state, out, guard, one, two, sums, total, matrix):
    matrix[...] = beside_matrix()

    def advance(src, dst, visit):
        main_sums(src, sums, matrix[...], (0, 1), SUBS, LIVE)

        def body(i, n, kind):
            shut = row_open(kind)
            load = lambda d: [[src[t, d, rows_at(i + j), :] for j in range(n)] for t in range(4)]
            before = center = load(0)
            for d in range(LAYERS):
                after = load(d + 1) if d + 1 < LAYERS else center
                around = []
                for t in range(4):
                    rows = beside_rows(lambda r, t=t, d=d: src[t, d, r, :], center[t], i, t % 2 == 1)
                    around.append(
                        [
                            (rows[j] + (before[t][j] + after[t][j])) + sums[t, d, rows_at(i + j), :]
                            for j in range(n)
                        ]
                    )
                for t in range(2):
                    for j in range(n):
                        at = rows_at(i + j)
                        scaled = NEUTRAL * center[t][j]
                        acid = RATE_ACID * around[t][j] + scaled * (1.0 - center[2 + t][j])
                        quench = RATE_QUENCH * around[2 + t][j] + center[2 + t][j] * (
                            (1.0 - 6.0 * RATE_QUENCH) - scaled
                        )
                        if kind != 1:
                            acid, quench = acid * shut, quench * shut
                        dst[t, d, at, :] = acid
                        dst[2 + t, d, at, :] = quench
                        if kind == 1:
                            visit(t, d, i + j, center[t][j], acid)
                before, center = center, after

        sweep(body)

    def begin(t, d, i, old, new):
        total[t, d, rows_at(i - 2), :] = old + new

    def protect(t, d, i, old, new):
        rows = rows_at(i - 2)
        guard[d, rows, pl.ds(t * LANES, LANES)] = jnp.exp(
            -DEPROTECT * (total[t, d, rows, :] + (old + new))
        )

    advance(state, one, begin)
    advance(one, two, lambda *_: None)
    advance(two, out, protect)


def run_main(role, state, *earlier):
    grid = (4, LAYERS, EXT, LANES)
    return pl.pallas_call(
        functools.partial(main_steps, role),
        in_specs=[VM] * (1 + len(earlier)),
        out_specs=[VM, VM],
        out_shape=[vmem(grid), vmem((LAYERS, ROWS, COLS))],
        input_output_aliases={1: 0, 2: 1} if earlier else {},
        scratch_shapes=[
            pltpu.VMEM(grid, F32),
            pltpu.VMEM(grid, F32),
            pltpu.VMEM(grid, F32),
            pltpu.VMEM((2, LAYERS, ROWS, LANES), F32),
            pltpu.VMEM((2 * COLS, COLS), jnp.bfloat16),
        ],
        compiler_params=params(28),
        cost_estimate=pl.CostEstimate(
            flops=(10**9, 1)[role], bytes_accessed=(3 * 10**7, 1)[role], transcendentals=0
        ),
        name=("main_early", "main_late")[role],
    )(state, *earlier)


def strip_sums(src, sums, matrices, fields):
    rows = pl.ds(SUBS, LIVE)
    for side in range(2):
        stacked = jnp.concatenate([src[2 * f + side, rows, :] for f in fields], 0)
        total = neighbour_sums([stacked], matrices[side])
        for n, f in enumerate(fields):
            sums[2 * f + side, rows, :] = total[n * LIVE : (n + 1) * LIVE]


def strip_open():
    gx = lax.axis_index("gx")
    place = iota(1) % GROUP
    left = jnp.where((place < HALO) & (gx == 0), 0.0, 1.0)
    right = jnp.where((place >= HALO) & (place < 2 * HALO) & (gx == lax.axis_size("gx") - 1), 0.0, 1.0)
    return left, right


def put_edges(target, i, left, right, visit):
    lane = iota(1)
    rows = rows_at(i - 2)
    place = lane % GROUP
    both = jnp.where((place >= HALO) & (place < 2 * HALO), left, right)
    for d in range(LAYERS):
        moved = shifted(both, -GROUP * d - HALO)
        for t in range(2):
            here = lane < HALO if t == 0 else lane >= LANES - HALO
            cols = pl.ds(t * LANES, LANES)
            value = jnp.where(here, moved, target[d, rows, cols])
            target[d, rows, cols] = value
            visit(d, t, value)


def strip_steps(edges, inner_in, up_in, down_in, guard_in, out, guard, density, one, two, sums, total, pooled):
    del guard_in
    even_col = lax.rem(lax.axis_index("gx"), 2) == 0
    early = is_early()
    place = iota(1) % GROUP
    opens = strip_open()
    matrices = strip_matrix(0), strip_matrix(HALO)
    for j in range(FOLD):
        outer = jnp.where(early, up_in[j], down_in[j])
        left = jnp.where(even_col, outer, inner_in[j])
        right = jnp.where(even_col, inner_in[j], outer)
        for m in range(4):
            rows = pl.ds(SUBS * (1 + j + FOLD * (m // 2)), SUBS)
            f = m % 2
            own = edges[f, rows, :]
            near = (place >= HALO) & (place < 2 * HALO)
            kept = jnp.where((place >= HALO) & (place < 3 * HALO), own, 0.0)
            one[2 * f, rows, :] = jnp.where(place < HALO, shifted(left, -4 * m), kept)
            kept = jnp.where((place < HALO) | (place >= 3 * HALO), own, 0.0)
            one[2 * f + 1, rows, :] = jnp.where(near, shifted(right, -4 * m), kept)

    def advance(src, dst, visit):
        strip_sums(src, sums, matrices, (0, 1))

        def body(i, n, kind):
            for side in range(2):
                shut = opens[side] * row_open(kind)
                for j in range(n):
                    rows = rows_at(i + j)
                    center = [src[2 * f + side, rows, :] for f in range(2)]
                    around = []
                    for f in range(2):
                        read = lambda r, f=f, side=side: src[2 * f + side, r, :]
                        beside = beside_rows(read, [center[f]], i + j, False)
                        around.append(beside[0] + sums[2 * f + side, rows, :])
                    scaled = NEUTRAL * center[0]
                    acid = RATE_ACID * around[0] + scaled * (1.0 - center[1])
                    quench = RATE_QUENCH * around[1] + center[1] * (
                        (1.0 - 6.0 * RATE_QUENCH) - scaled
                    )
                    acid = acid * shut
                    dst[side, rows, :] = acid
                    dst[2 + side, rows, :] = quench * shut
                    visit(side, rows, center[0], acid)

        sweep(body)

    def begin(side, rows, old, new):
        total[side, rows, :] = old + new

    def protect(side, rows, old, new):
        total[side, rows, :] = jnp.exp(-DEPROTECT * (total[side, rows, :] + (old + new)))

    advance(one, two, begin)
    advance(two, one, lambda *_: None)
    advance(one, out, protect)

    def merge(i, _):
        kept = [None, None]

        def add(d, t, value):
            kept[t] = value if d == 0 else kept[t] + value

        put_edges(guard, i, total[0, rows_at(i), :], total[1, rows_at(i), :], add)
        for t in range(2):
            pooled[rows_at(i - 2), pl.ds(t * LANES, LANES)] = kept[t]
        return 0

    lax.fori_loop(2, 2 + RUN, merge, 0, unroll=8)
    fine = pooled[...].reshape(TILE, COARSEN, COLS).sum(1)
    col = lax.broadcasted_iota(jnp.int32, (COLS, LANES), 0)
    block = lax.broadcasted_iota(jnp.int32, (COLS, LANES), 1)
    pool = (col // COARSEN == block).astype(F32)
    coarse = jnp.dot(fine, pool, precision=lax.Precision.HIGHEST, preferred_element_type=F32)
    wide = lax.broadcasted_iota(jnp.int32, (TILE, LANES), 1)
    mean = 1.0 - coarse * (1.0 / (LAYERS * COARSEN * COARSEN))
    density[...] = jnp.where(wide < TILE, mean, 0.0)


def run_strips(edges, inner, up, down, guard):
    edge = (4, EXT, LANES)
    whole = (LAYERS, ROWS, COLS)
    return pl.pallas_call(
        strip_steps,
        in_specs=[VM] * 5,
        out_specs=[VM] * 3,
        out_shape=[vmem(edge), vmem(whole), jax.ShapeDtypeStruct((TILE, LANES), F32)],
        input_output_aliases={4: 1},
        scratch_shapes=[
            pltpu.VMEM(edge, F32),
            pltpu.VMEM(edge, F32),
            pltpu.VMEM(edge, F32),
            pltpu.VMEM((2, EXT, LANES), F32),
            pltpu.VMEM((ROWS, COLS), F32),
        ],
        compiler_params=params(8),
        name="strip_steps",
    )(edges, inner, up, down, guard)


def last_step(
    state, strips, guard, col_ref, acid_out, guard_out, cols, sums, edge_sums, matrix, land, sems
):
    kept = pltpu.make_async_copy(guard, guard_out, sems.at[PARTS])
    kept.start()
    matrix[...] = beside_matrix()
    main_sums(state, sums, matrix[...], (0,), BASE, ROWS)
    strip_sums(strips, edge_sums, (strip_matrix(0), strip_matrix(HALO)), (0,))
    n = BATCH

    def body(p, _):
        i = 2 + p * n
        for t in range(2):
            load = lambda d, t=t: [state[t, d, rows_at(i + j), :] for j in range(n)]
            before = center = load(0)
            for d in range(LAYERS):
                after = load(d + 1) if d + 1 < LAYERS else center
                rows = beside_rows(lambda r, t=t, d=d: state[t, d, r, :], center, i, t == 1)
                for j in range(n):
                    at = rows_at(i + j)
                    around = (rows[j] + (before[j] + after[j])) + sums[t, d, at, :]
                    land[d, rows_at(i + j - 2), pl.ds(t * LANES, LANES)] = RATE_ACID * around + (
                        NEUTRAL * center[j]
                    ) * (1.0 - state[2 + t, d, at, :])
                before, center = center, after
        for j in range(n):
            at = rows_at(i + j)
            edges = []
            for side in range(2):
                center = strips[side, at, :]
                beside = beside_rows(lambda r, side=side: strips[side, r, :], [center], i + j, False)
                around = beside[0] + edge_sums[side, at, :]
                edges.append(
                    RATE_ACID * around + (NEUTRAL * center) * (1.0 - strips[2 + side, at, :])
                )
            put_edges(land, i + j, *edges, lambda *_: None)
        return 0

    size = ROWS // PARTS
    copies = []
    for p in range(PARTS):
        count = size // SUBS // n
        lax.fori_loop(p * count, (p + 1) * count, body, 0)
        part = pl.ds(size * p, size)
        copies.append(pltpu.make_async_copy(land.at[:, part, :], acid_out.at[:, part, :], sems.at[p]))
        copies[p].start()
    for m, offset in enumerate(tile_offsets()):
        start = pl.multiple_of((offset + 3) * TILE, TILE)
        cols[pl.ds(TILE * m, TILE), :] = col_ref[pl.ds(start, TILE), :]
    for copy in copies:
        copy.wait()
    kept.wait()


def run_last(state, strips, guard):
    whole = jax.ShapeDtypeStruct((LAYERS, ROWS, COLS), F32)
    return pl.pallas_call(
        last_step,
        in_specs=[VM] * 4,
        out_specs=[HB, HB, VM],
        out_shape=[whole, whole, vmem((6 * TILE, LANES))],
        scratch_shapes=[
            pltpu.VMEM((2, LAYERS, EXT, LANES), F32),
            pltpu.VMEM((2, EXT, LANES), F32),
            pltpu.VMEM((2 * COLS, COLS), jnp.bfloat16),
            pltpu.VMEM((LAYERS, ROWS, COLS), F32),
            pltpu.SemaphoreType.DMA((PARTS + 1,)),
        ],
        compiler_params=params(12),
        cost_estimate=pl.CostEstimate(flops=10**9, bytes_accessed=10**7, transcendentals=0),
        name="last_step",
    )(state, strips, guard, jnp.asarray(column_table()))


def weights(distance):
    offset = np.arange(-REACH, REACH + 1, dtype=np.float64)
    norm = np.exp(-offset * offset / (2.0 * SPREAD * SPREAD)).sum()
    value = np.exp(-(distance.astype(np.float64) ** 2) / (2.0 * SPREAD * SPREAD))
    return np.where(np.abs(distance) <= REACH, value / norm, 0.0).astype(np.float32)


def row_table():
    me = np.arange(4)[:, None, None, None]
    k = np.arange(4)[None, :, None, None]
    i = np.arange(TILE)[None, None, :, None]
    p = np.arange(TILE)[None, None, None, :]
    return weights(TILE * ((me ^ k) - me) + p - i).reshape(4, 4 * TILE, TILE)


def column_table():
    c = np.arange(7 * TILE)[:, None] - 3 * TILE
    j = np.arange(LANES)[None, :]
    return np.where(j < TILE, weights(c - j), np.float32(0.0))


def tile_offsets():
    gx = lax.axis_index("gx")
    beside = 1 - 2 * lax.rem(gx, 2)
    step = 2 - 4 * lax.rem(lax.div(gx, 2), 2)
    return [0 * gx, beside, step, step + beside, -step, -step + beside]


def product(a, b):
    return jnp.dot(a, b, precision=lax.Precision.HIGHEST, preferred_element_type=F32)


def mix_columns(pair, near, far, cols, out):
    total = product(pair[...], cols[pl.ds(0, 2 * TILE), :])
    total += product(near[...], cols[pl.ds(2 * TILE, 2 * TILE), :])
    out[...] = total + product(far[...], cols[pl.ds(4 * TILE, 2 * TILE), :])


def run_mix(pair, near, far, cols):
    return pl.pallas_call(
        mix_columns,
        in_specs=[VM] * 4,
        out_specs=VM,
        out_shape=jax.ShapeDtypeStruct((TILE, LANES), F32),
        compiler_params=params(4),
        name="mix_columns",
    )(pair, near, far, cols)


def etch(low, high, guard, row_ref, out):
    gy = lax.axis_index("gy")
    every = jnp.concatenate([low[...], high[...]], 1)
    rows = product(row_ref[gy], every)
    k = lax.broadcasted_iota(jnp.int32, rows.shape, 0) // TILE
    rows = jnp.where(k == lax.broadcasted_iota(jnp.int32, rows.shape, 1) // TILE, rows, 0.0)
    rows = sum(rows[TILE * n : TILE * (n + 1)] for n in range(4))
    j = lax.broadcasted_iota(jnp.int32, (LANES, COLS), 0) % TILE
    widen = (j == lax.broadcasted_iota(jnp.int32, (LANES, COLS), 1) // COARSEN).astype(F32)
    smooth = product(rows, widen)
    factor = 1.0 - LOADING * smooth
    for i in range(TILE):
        rows = pl.ds(COARSEN * i, COARSEN)
        for t in range(2):
            piece = factor[i : i + 1, t * LANES : (t + 1) * LANES]
            cols_of = pl.ds(t * LANES, LANES)
            out[rows, cols_of] = (1.0 - guard[0, rows, cols_of]) * piece


def run_etch(low, high, guard):
    return pl.pallas_call(
        etch,
        in_specs=[VM] * 4,
        out_specs=VM,
        out_shape=jax.ShapeDtypeStruct((ROWS, COLS), F32),
        compiler_params=params(4),
        name="etch",
    )(low, high, guard, jnp.asarray(row_table()))


def swap(block, axis, partner):
    count = lax.axis_size(axis)
    route = [(i, partner(i)) for i in range(count) if 0 <= partner(i) < count]
    return lax.ppermute(block, axis, route)


def inside(i):
    return i ^ 1


def outside(i):
    return i - 1 if i % 2 == 0 else i + 1


def shift(block, axis, early):
    count = lax.axis_size(axis)
    route = [(i, outside(i)) for i in range(count) if early_column(i) == early]
    return lax.ppermute(block, axis, [(i, k) for i, k in route if 0 <= k < count])


def shards(acid_field, quencher_field):
    acid_field = pltpu.with_memory_space_constraint(acid_field, pltpu.HBM)
    quencher_field = pltpu.with_memory_space_constraint(quencher_field, pltpu.HBM)
    first, second = pack_rows(acid_field, quencher_field)
    second = swap(second, "gy", outside)
    first = swap(first, "gy", inside)
    state, edges = load_state(acid_field, quencher_field)
    state, edges, second, first = pack_columns(state, edges, second, first)
    inner = swap(first, "gx", inside)
    up = shift(second, "gx", 0)
    state_early, guard = run_main(0, state)
    second, state_early = lax.optimization_barrier((second, state_early))
    down = shift(second, "gx", 1)
    up, inner, state_early = lax.optimization_barrier((up, inner, state_early))
    state, guard = run_main(1, state, state_early, guard)
    strips, guard, density = run_strips(edges, inner, up, down, guard)
    tile = density[:, :TILE]
    pair = jnp.concatenate([tile, swap(tile, "gx", inside)], 1)
    far = swap(pair, "gx", lambda i: i - 2 if i // 2 % 2 == 0 else i + 2)
    near = swap(pair, "gx", lambda i: i ^ 2)
    acid_after, inhibitor, cols = run_last(state, strips, guard)
    near, far, cols = lax.optimization_barrier((near, far, cols))
    mixed = run_mix(pair, near, far, cols)[:, :TILE]
    low = jnp.concatenate([mixed, swap(mixed, "gy", lambda i: i ^ 1)], 1)
    high = swap(low, "gy", lambda i: i ^ 2)
    etch_rate = run_etch(low, high, guard)
    return acid_after, inhibitor, etch_rate


def solution(mesh):
    in_specs = (P(None, "gy", "gx"), P(None, "gy", "gx"))
    out_specs = (P(None, "gy", "gx"), P(None, "gy", "gx"), P("gy", "gx"))
    return jax.shard_map(shards, mesh=mesh, in_specs=in_specs, out_specs=out_specs, check_vma=False)
```

```python
import functools

import jax
import jax.numpy as jnp
import numpy as np
from jax import lax
from jax.experimental import pallas as pl
from jax.experimental.pallas import tpu as pltpu
from jax.sharding import PartitionSpec as P

RATE_ACID = 0.15
RATE_QUENCH = 0.05
NEUTRAL = 0.1
DEPROTECT = 0.35
LOADING = 0.8
STEPS = 4
COARSEN = 8
REACH = 64
SPREAD = 25.0

LAYERS = 8
ROWS = 256
COLS = 256
LANES = 128
SUBS = 8
RUN = ROWS // SUBS
HALO = STEPS
BASE = 2 * SUBS
EXT = ROWS + 2 * BASE
LIVE = ROWS + BASE
FOLD = LIVE // SUBS // 2
PARTS = 4
TILE = ROWS // COARSEN
BATCH = 4
GROUP = 16

VM = pl.BlockSpec(memory_space=pltpu.VMEM)
HB = pl.BlockSpec(memory_space=pltpu.HBM)
F32 = jnp.float32


def params(mib):
    return pltpu.CompilerParams(vmem_limit_bytes=mib * 1024 * 1024)


EARLY_COLUMNS = (0, 1, 4, 6)
PERIOD = 8


def early_column(i):
    return sum((i % PERIOD == k) * 1 for k in EARLY_COLUMNS)


def is_early():
    place = lax.rem(lax.axis_index("gx"), PERIOD)
    return functools.reduce(jnp.logical_or, [place == k for k in EARLY_COLUMNS])


def vmem(shape):
    return pltpu.VMEM(shape, F32)


def iota(dim):
    return lax.broadcasted_iota(jnp.int32, (SUBS, LANES), dim)


def row_strips(a_top, a_bot, q_top, q_bot, first_ref, second_ref):
    even = lax.rem(lax.axis_index("gy"), 2) == 0
    low = lax.broadcasted_iota(jnp.int32, (SUBS, COLS), 0) < HALO
    for d in range(LAYERS):
        top = jnp.where(low, a_top[d], pltpu.roll(q_top[d], HALO, 0))
        bot = jnp.where(low, pltpu.roll(a_bot[d], HALO, 0), q_bot[d])
        first_ref[d] = jnp.where(even, bot, top)
        second_ref[d] = jnp.where(even, top, bot)


def pack_rows(acid, quench):
    block = (LAYERS, SUBS, COLS)
    top = pl.BlockSpec(block, lambda i: (0, 0, 0))
    bot = pl.BlockSpec(block, lambda i: (0, RUN - 1, 0))
    out = jax.ShapeDtypeStruct(block, F32)
    return pl.pallas_call(
        row_strips,
        grid=(1,),
        in_specs=[top, bot, top, bot],
        out_specs=[pl.BlockSpec(block, lambda i: (0, 0, 0))] * 2,
        out_shape=[out, out],
        compiler_params=params(4),
        name="pack_rows",
    )(acid, acid, quench, quench)


def shifted(x, by):
    return pltpu.roll(x, by % LANES, 1)


def rows_at(i):
    return pl.ds(pl.multiple_of(i * SUBS, SUBS), SUBS)


def own_edges(state, edges, i):
    lane = iota(1)
    rows = rows_at(i)
    for f in range(2):
        total = None
        for d in range(LAYERS):
            first = jnp.where(lane < 2 * HALO, state[2 * f, d, rows, :], 0.0)
            both = jnp.where(lane >= LANES - 2 * HALO, state[2 * f + 1, d, rows, :], first)
            moved = shifted(both, GROUP * d + HALO)
            total = moved if d == 0 else total + moved
        edges[f, rows, :] = total


def fill_state(acid, quench, state, edges, sems):
    size = ROWS // PARTS
    copies = []
    for p in range(PARTS):
        for t in range(4):
            source = (acid, quench)[t // 2].at[
                :, pl.ds(size * p, size), pl.ds((t % 2) * LANES, LANES)
            ]
            target = state.at[t, :, pl.ds(BASE + size * p, size), :]
            copy = pltpu.make_async_copy(source, target, sems.at[p, t])
            copy.start()
            copies.append(copy)
    for p in range(PARTS):
        for t in range(4):
            copies[4 * p + t].wait()

        def body(i, _):
            own_edges(state, edges, i)
            return 0

        first = (BASE + size * p) // SUBS
        lax.fori_loop(first, first + size // SUBS, body, 0, unroll=4)


def load_state(acid, quench):
    return pl.pallas_call(
        fill_state,
        in_specs=[HB, HB],
        out_specs=[VM, VM],
        out_shape=[vmem((4, LAYERS, EXT, LANES)), vmem((2, EXT, LANES))],
        scratch_shapes=[pltpu.SemaphoreType.DMA((PARTS, 4))],
        compiler_params=params(4),
        name="load_state",
    )(acid, quench)


def column_strips(state_in, edges_in, second_in, first_in, state, edges, second_ref, first_ref):
    del state_in, edges_in
    even_row = lax.rem(lax.axis_index("gy"), 2) == 0
    even_col = lax.rem(lax.axis_index("gx"), 2) == 0
    sub = iota(0)
    place = iota(1) % GROUP
    for d in range(LAYERS):
        for t in range(2):
            cols = pl.ds(t * LANES, LANES)
            one, two = first_in[d, :, cols], second_in[d, :, cols]
            top = jnp.where(even_row, two, one)
            bot = jnp.where(even_row, one, two)
            above, below = pl.ds(SUBS, SUBS), pl.ds(BASE + ROWS, SUBS)
            state[t, d, above, :] = jnp.where(sub >= HALO, pltpu.roll(top, HALO, 0), 0.0)
            state[2 + t, d, above, :] = jnp.where(sub >= HALO, top, 0.0)
            state[t, d, below, :] = jnp.where(sub < HALO, bot, 0.0)
            state[2 + t, d, below, :] = jnp.where(sub < HALO, pltpu.roll(bot, HALO, 0), 0.0)
    own_edges(state, edges, 1)
    own_edges(state, edges, (BASE + ROWS) // SUBS)
    for j in range(FOLD):
        left = jnp.zeros((SUBS, LANES), F32)
        right = jnp.zeros((SUBS, LANES), F32)
        for m in range(4):
            rows = pl.ds(SUBS * (1 + j + FOLD * (m // 2)), SUBS)
            moved = shifted(edges[m % 2, rows, :], 4 * m)
            left = jnp.where((place - HALO - 4 * m) % GROUP < HALO, moved, left)
            right = jnp.where((place - 4 * m) % GROUP < HALO, moved, right)
        first_ref[j] = jnp.where(even_col, right, left)
        second_ref[j] = jnp.where(even_col, left, right)


def pack_columns(state, edges, second, first):
    strip = jax.ShapeDtypeStruct((FOLD, SUBS, LANES), F32)
    return pl.pallas_call(
        column_strips,
        in_specs=[VM] * 4,
        out_specs=[VM] * 4,
        out_shape=[vmem((4, LAYERS, EXT, LANES)), vmem((2, EXT, LANES)), strip, strip],
        input_output_aliases={0: 0, 1: 1},
        compiler_params=params(4),
        name="pack_columns",
    )(state, edges, second, first)


def halves(x):
    high = x.astype(jnp.bfloat16)
    return high, (x - high.astype(F32)).astype(jnp.bfloat16)


def neighbour_sums(parts, matrix):
    split = [halves(x) for x in parts]
    stacked = jnp.concatenate([h for h, _ in split] + [l for _, l in split], 1)
    return jnp.dot(stacked, matrix, preferred_element_type=F32)


def beside_matrix():
    shape = (2 * COLS, COLS)
    row = lax.broadcasted_iota(jnp.int32, shape, 0) % COLS
    col = lax.broadcasted_iota(jnp.int32, shape, 1)
    return (jnp.abs(row - col) == 1).astype(jnp.bfloat16)


def strip_matrix(offset):
    shape = (2 * LANES, LANES)
    row = lax.broadcasted_iota(jnp.int32, shape, 0) % LANES
    col = lax.broadcasted_iota(jnp.int32, shape, 1)
    layer = ((col + offset) % LANES) // GROUP
    gap = (row - col + LANES) % LANES
    beside = ((gap == 1) | (gap == LANES - 1)).astype(F32)
    lower = (gap == jnp.where(layer == 0, 0, LANES - GROUP)).astype(F32)
    upper = (gap == jnp.where(layer == LAYERS - 1, 0, GROUP)).astype(F32)
    return (beside + lower + upper).astype(jnp.bfloat16)


def row_open(kind):
    gy = lax.axis_index("gy")
    if kind == 1:
        return 1.0
    outside = gy == 0 if kind == 0 else gy == lax.axis_size("gy") - 1
    return 1.0 - outside.astype(jnp.int32).astype(F32)


def sweep(body):
    def step(p, _):
        body(2 + p * BATCH, BATCH, 1)
        return 0

    body(1, 1, 0)
    lax.fori_loop(0, RUN // BATCH, step, 0)
    body(2 + RUN, 1, 2)


def beside_rows(read, center, i, mixed):
    n = len(center)
    above = [read(pl.ds((i + j) * SUBS - 1, SUBS)) for j in range(n)]
    if not mixed:
        return [above[j] + read(pl.ds((i + j) * SUBS + 1, SUBS)) for j in range(n)]
    last = iota(0) == SUBS - 1
    up = [pltpu.roll(x, SUBS - 1, 0) for x in center + [read(rows_at(i + n))]]
    return [above[j] + jnp.where(last, up[j + 1], up[j]) for j in range(n)]


def main_sums(src, sums, matrix, fields, start, count):
    for f in fields:
        parts = [src[2 * f + t, :, pl.ds(start, count), :].reshape(LAYERS * count, LANES) for t in range(2)]
        total = neighbour_sums(parts, matrix)
        for t in range(2):
            piece = total[:, t * LANES : (t + 1) * LANES].reshape(LAYERS, count, LANES)
            sums[2 * f + t, :, pl.ds(start, count), :] = piece


def main_steps(role, state, *refs):
    out, guard, one, two, sums, total, matrix = refs[-7:]

    @pl.when(is_early() == (role == 0))
    def _():
        main_part(state, out, guard, one, two, sums, total, matrix)


def main_part(state, out, guard, one, two, sums, total, matrix):
    matrix[...] = beside_matrix()

    def advance(src, dst, visit):
        main_sums(src, sums, matrix[...], (0, 1), SUBS, LIVE)

        def body(i, n, kind):
            shut = row_open(kind)
            load = lambda d: [[src[t, d, rows_at(i + j), :] for j in range(n)] for t in range(4)]
            before = center = load(0)
            for d in range(LAYERS):
                after = load(d + 1) if d + 1 < LAYERS else center
                around = []
                for t in range(4):
                    rows = beside_rows(lambda r, t=t, d=d: src[t, d, r, :], center[t], i, t % 2 == 1)
                    around.append(
                        [
                            (rows[j] + (before[t][j] + after[t][j])) + sums[t, d, rows_at(i + j), :]
                            for j in range(n)
                        ]
                    )
                for t in range(2):
                    for j in range(n):
                        at = rows_at(i + j)
                        scaled = NEUTRAL * center[t][j]
                        acid = RATE_ACID * around[t][j] + scaled * (1.0 - center[2 + t][j])
                        quench = RATE_QUENCH * around[2 + t][j] + center[2 + t][j] * (
                            (1.0 - 6.0 * RATE_QUENCH) - scaled
                        )
                        if kind != 1:
                            acid, quench = acid * shut, quench * shut
                        dst[t, d, at, :] = acid
                        dst[2 + t, d, at, :] = quench
                        if kind == 1:
                            visit(t, d, i + j, center[t][j], acid)
                before, center = center, after

        sweep(body)

    def begin(t, d, i, old, new):
        total[t, d, rows_at(i - 2), :] = old + new

    def protect(t, d, i, old, new):
        rows = rows_at(i - 2)
        guard[d, rows, pl.ds(t * LANES, LANES)] = jnp.exp(
            -DEPROTECT * (total[t, d, rows, :] + (old + new))
        )

    advance(state, one, begin)
    advance(one, two, lambda *_: None)
    advance(two, out, protect)


def run_main(role, state, *earlier):
    grid = (4, LAYERS, EXT, LANES)
    return pl.pallas_call(
        functools.partial(main_steps, role),
        in_specs=[VM] * (1 + len(earlier)),
        out_specs=[VM, VM],
        out_shape=[vmem(grid), vmem((LAYERS, ROWS, COLS))],
        input_output_aliases={1: 0, 2: 1} if earlier else {},
        scratch_shapes=[
            pltpu.VMEM(grid, F32),
            pltpu.VMEM(grid, F32),
            pltpu.VMEM(grid, F32),
            pltpu.VMEM((2, LAYERS, ROWS, LANES), F32),
            pltpu.VMEM((2 * COLS, COLS), jnp.bfloat16),
        ],
        compiler_params=params(28),
        cost_estimate=pl.CostEstimate(
            flops=(10**9, 1)[role], bytes_accessed=(3 * 10**7, 1)[role], transcendentals=0
        ),
        name=("main_early", "main_late")[role],
    )(state, *earlier)


def strip_sums(src, sums, matrices, fields):
    rows = pl.ds(SUBS, LIVE)
    for side in range(2):
        stacked = jnp.concatenate([src[2 * f + side, rows, :] for f in fields], 0)
        total = neighbour_sums([stacked], matrices[side])
        for n, f in enumerate(fields):
            sums[2 * f + side, rows, :] = total[n * LIVE : (n + 1) * LIVE]


def strip_open():
    gx = lax.axis_index("gx")
    place = iota(1) % GROUP
    left = jnp.where((place < HALO) & (gx == 0), 0.0, 1.0)
    right = jnp.where((place >= HALO) & (place < 2 * HALO) & (gx == lax.axis_size("gx") - 1), 0.0, 1.0)
    return left, right


def put_edges(target, i, left, right, visit):
    lane = iota(1)
    rows = rows_at(i - 2)
    place = lane % GROUP
    both = jnp.where((place >= HALO) & (place < 2 * HALO), left, right)
    for d in range(LAYERS):
        moved = shifted(both, -GROUP * d - HALO)
        for t in range(2):
            here = lane < HALO if t == 0 else lane >= LANES - HALO
            cols = pl.ds(t * LANES, LANES)
            value = jnp.where(here, moved, target[d, rows, cols])
            target[d, rows, cols] = value
            visit(d, t, value)


def strip_steps(edges, inner_in, up_in, down_in, guard_in, out, guard, density, one, two, sums, total, pooled):
    del guard_in
    even_col = lax.rem(lax.axis_index("gx"), 2) == 0
    early = is_early()
    place = iota(1) % GROUP
    opens = strip_open()
    matrices = strip_matrix(0), strip_matrix(HALO)
    for j in range(FOLD):
        outer = jnp.where(early, up_in[j], down_in[j])
        left = jnp.where(even_col, outer, inner_in[j])
        right = jnp.where(even_col, inner_in[j], outer)
        for m in range(4):
            rows = pl.ds(SUBS * (1 + j + FOLD * (m // 2)), SUBS)
            f = m % 2
            own = edges[f, rows, :]
            near = (place >= HALO) & (place < 2 * HALO)
            kept = jnp.where((place >= HALO) & (place < 3 * HALO), own, 0.0)
            one[2 * f, rows, :] = jnp.where(place < HALO, shifted(left, -4 * m), kept)
            kept = jnp.where((place < HALO) | (place >= 3 * HALO), own, 0.0)
            one[2 * f + 1, rows, :] = jnp.where(near, shifted(right, -4 * m), kept)

    def advance(src, dst, visit):
        strip_sums(src, sums, matrices, (0, 1))

        def body(i, n, kind):
            for side in range(2):
                shut = opens[side] * row_open(kind)
                for j in range(n):
                    rows = rows_at(i + j)
                    center = [src[2 * f + side, rows, :] for f in range(2)]
                    around = []
                    for f in range(2):
                        read = lambda r, f=f, side=side: src[2 * f + side, r, :]
                        beside = beside_rows(read, [center[f]], i + j, False)
                        around.append(beside[0] + sums[2 * f + side, rows, :])
                    scaled = NEUTRAL * center[0]
                    acid = RATE_ACID * around[0] + scaled * (1.0 - center[1])
                    quench = RATE_QUENCH * around[1] + center[1] * (
                        (1.0 - 6.0 * RATE_QUENCH) - scaled
                    )
                    acid = acid * shut
                    dst[side, rows, :] = acid
                    dst[2 + side, rows, :] = quench * shut
                    visit(side, rows, center[0], acid)

        sweep(body)

    def begin(side, rows, old, new):
        total[side, rows, :] = old + new

    def protect(side, rows, old, new):
        total[side, rows, :] = jnp.exp(-DEPROTECT * (total[side, rows, :] + (old + new)))

    advance(one, two, begin)
    advance(two, one, lambda *_: None)
    advance(one, out, protect)

    def merge(i, _):
        kept = [None, None]

        def add(d, t, value):
            kept[t] = value if d == 0 else kept[t] + value

        put_edges(guard, i, total[0, rows_at(i), :], total[1, rows_at(i), :], add)
        for t in range(2):
            pooled[rows_at(i - 2), pl.ds(t * LANES, LANES)] = kept[t]
        return 0

    lax.fori_loop(2, 2 + RUN, merge, 0, unroll=8)
    fine = pooled[...].reshape(TILE, COARSEN, COLS).sum(1)
    col = lax.broadcasted_iota(jnp.int32, (COLS, LANES), 0)
    block = lax.broadcasted_iota(jnp.int32, (COLS, LANES), 1)
    pool = (col // COARSEN == block).astype(jnp.bfloat16)
    high, low = halves(fine)
    coarse = jnp.dot(high, pool, preferred_element_type=F32) + jnp.dot(
        low, pool, preferred_element_type=F32
    )
    wide = lax.broadcasted_iota(jnp.int32, (TILE, LANES), 1)
    mean = 1.0 - coarse * (1.0 / (LAYERS * COARSEN * COARSEN))
    density[...] = jnp.where(wide < TILE, mean, 0.0)


def run_strips(edges, inner, up, down, guard):
    edge = (4, EXT, LANES)
    whole = (LAYERS, ROWS, COLS)
    return pl.pallas_call(
        strip_steps,
        in_specs=[VM] * 5,
        out_specs=[VM] * 3,
        out_shape=[vmem(edge), vmem(whole), jax.ShapeDtypeStruct((TILE, LANES), F32)],
        input_output_aliases={4: 1},
        scratch_shapes=[
            pltpu.VMEM(edge, F32),
            pltpu.VMEM(edge, F32),
            pltpu.VMEM(edge, F32),
            pltpu.VMEM((2, EXT, LANES), F32),
            pltpu.VMEM((ROWS, COLS), F32),
        ],
        compiler_params=params(8),
        name="strip_steps",
    )(edges, inner, up, down, guard)


def last_step(
    state, strips, guard, col_ref, acid_out, guard_out, cols, sums, edge_sums, matrix, land, sems
):
    kept = pltpu.make_async_copy(guard, guard_out, sems.at[PARTS])
    kept.start()
    matrix[...] = beside_matrix()
    main_sums(state, sums, matrix[...], (0,), BASE, ROWS)
    strip_sums(strips, edge_sums, (strip_matrix(0), strip_matrix(HALO)), (0,))
    n = BATCH

    def body(p, _):
        i = 2 + p * n
        for t in range(2):
            load = lambda d, t=t: [state[t, d, rows_at(i + j), :] for j in range(n)]
            before = center = load(0)
            for d in range(LAYERS):
                after = load(d + 1) if d + 1 < LAYERS else center
                rows = beside_rows(lambda r, t=t, d=d: state[t, d, r, :], center, i, t == 1)
                for j in range(n):
                    at = rows_at(i + j)
                    around = (rows[j] + (before[j] + after[j])) + sums[t, d, at, :]
                    land[d, rows_at(i + j - 2), pl.ds(t * LANES, LANES)] = RATE_ACID * around + (
                        NEUTRAL * center[j]
                    ) * (1.0 - state[2 + t, d, at, :])
                before, center = center, after
        for j in range(n):
            at = rows_at(i + j)
            edges = []
            for side in range(2):
                center = strips[side, at, :]
                beside = beside_rows(lambda r, side=side: strips[side, r, :], [center], i + j, False)
                around = beside[0] + edge_sums[side, at, :]
                edges.append(
                    RATE_ACID * around + (NEUTRAL * center) * (1.0 - strips[2 + side, at, :])
                )
            put_edges(land, i + j, *edges, lambda *_: None)
        return 0

    size = ROWS // PARTS
    copies = []
    for p in range(PARTS):
        count = size // SUBS // n
        lax.fori_loop(p * count, (p + 1) * count, body, 0)
        part = pl.ds(size * p, size)
        copies.append(pltpu.make_async_copy(land.at[:, part, :], acid_out.at[:, part, :], sems.at[p]))
        copies[p].start()
    for m, offset in enumerate(tile_offsets()):
        start = pl.multiple_of((offset + 3) * TILE, TILE)
        cols[pl.ds(TILE * m, TILE), :] = col_ref[pl.ds(start, TILE), :]
    for copy in copies:
        copy.wait()
    kept.wait()


def run_last(state, strips, guard):
    whole = jax.ShapeDtypeStruct((LAYERS, ROWS, COLS), F32)
    return pl.pallas_call(
        last_step,
        in_specs=[VM] * 4,
        out_specs=[HB, HB, VM],
        out_shape=[whole, whole, vmem((6 * TILE, LANES))],
        scratch_shapes=[
            pltpu.VMEM((2, LAYERS, EXT, LANES), F32),
            pltpu.VMEM((2, EXT, LANES), F32),
            pltpu.VMEM((2 * COLS, COLS), jnp.bfloat16),
            pltpu.VMEM((LAYERS, ROWS, COLS), F32),
            pltpu.SemaphoreType.DMA((PARTS + 1,)),
        ],
        compiler_params=params(12),
        cost_estimate=pl.CostEstimate(flops=10**9, bytes_accessed=10**7, transcendentals=0),
        name="last_step",
    )(state, strips, guard, jnp.asarray(column_table()))


def weights(distance):
    offset = np.arange(-REACH, REACH + 1, dtype=np.float64)
    norm = np.exp(-offset * offset / (2.0 * SPREAD * SPREAD)).sum()
    value = np.exp(-(distance.astype(np.float64) ** 2) / (2.0 * SPREAD * SPREAD))
    return np.where(np.abs(distance) <= REACH, value / norm, 0.0).astype(np.float32)


def row_table():
    me = np.arange(4)[:, None, None, None]
    k = np.arange(4)[None, :, None, None]
    i = np.arange(TILE)[None, None, :, None]
    p = np.arange(TILE)[None, None, None, :]
    return weights(TILE * ((me ^ k) - me) + p - i).reshape(4, 4 * TILE, TILE)


def column_table():
    c = np.arange(7 * TILE)[:, None] - 3 * TILE
    j = np.arange(LANES)[None, :]
    return np.where(j < TILE, weights(c - j), np.float32(0.0))


def tile_offsets():
    gx = lax.axis_index("gx")
    beside = 1 - 2 * lax.rem(gx, 2)
    step = 2 - 4 * lax.rem(lax.div(gx, 2), 2)
    return [0 * gx, beside, step, step + beside, -step, -step + beside]


def product(a, b):
    a_high, a_low = halves(a)
    b_high, b_low = halves(b)
    dot = functools.partial(jnp.dot, preferred_element_type=F32)
    return dot(a_high, b_high) + (dot(a_low, b_high) + dot(a_high, b_low))


def mix_columns(pair, near, far, cols, out):
    total = product(pair[...], cols[pl.ds(0, 2 * TILE), :])
    total += product(near[...], cols[pl.ds(2 * TILE, 2 * TILE), :])
    out[...] = total + product(far[...], cols[pl.ds(4 * TILE, 2 * TILE), :])


def run_mix(pair, near, far, cols):
    return pl.pallas_call(
        mix_columns,
        in_specs=[VM] * 4,
        out_specs=VM,
        out_shape=jax.ShapeDtypeStruct((TILE, LANES), F32),
        compiler_params=params(4),
        name="mix_columns",
    )(pair, near, far, cols)


def etch(near_in, far_in, guard, row_ref, out):
    gy = lax.axis_index("gy")
    every = jnp.concatenate([near_in[...], far_in[...]], 1)
    rows = product(row_ref[gy], every)
    k = lax.broadcasted_iota(jnp.int32, rows.shape, 0) // TILE
    rows = jnp.where(k == lax.broadcasted_iota(jnp.int32, rows.shape, 1) // TILE, rows, 0.0)
    rows = sum(rows[TILE * n : TILE * (n + 1)] for n in range(4))
    j = lax.broadcasted_iota(jnp.int32, (LANES, COLS), 0) % TILE
    widen = (j == lax.broadcasted_iota(jnp.int32, (LANES, COLS), 1) // COARSEN).astype(F32)
    high, low = halves(rows)
    widen = widen.astype(jnp.bfloat16)
    smooth = jnp.dot(high, widen, preferred_element_type=F32) + jnp.dot(
        low, widen, preferred_element_type=F32
    )
    factor = 1.0 - LOADING * smooth
    for i in range(TILE):
        rows = pl.ds(COARSEN * i, COARSEN)
        for t in range(2):
            piece = factor[i : i + 1, t * LANES : (t + 1) * LANES]
            cols_of = pl.ds(t * LANES, LANES)
            out[rows, cols_of] = (1.0 - guard[0, rows, cols_of]) * piece


def run_etch(low, high, guard):
    return pl.pallas_call(
        etch,
        in_specs=[VM] * 4,
        out_specs=VM,
        out_shape=jax.ShapeDtypeStruct((ROWS, COLS), F32),
        compiler_params=params(4),
        name="etch",
    )(low, high, guard, jnp.asarray(row_table()))


def swap(block, axis, partner):
    count = lax.axis_size(axis)
    route = [(i, partner(i)) for i in range(count) if 0 <= partner(i) < count]
    return lax.ppermute(block, axis, route)


def inside(i):
    return i ^ 1


def outside(i):
    return i - 1 if i % 2 == 0 else i + 1


def shift(block, axis, early):
    count = lax.axis_size(axis)
    route = [(i, outside(i)) for i in range(count) if early_column(i) == early]
    return lax.ppermute(block, axis, [(i, k) for i, k in route if 0 <= k < count])


def shards(acid_field, quencher_field):
    acid_field = pltpu.with_memory_space_constraint(acid_field, pltpu.HBM)
    quencher_field = pltpu.with_memory_space_constraint(quencher_field, pltpu.HBM)
    first, second = pack_rows(acid_field, quencher_field)
    second = swap(second, "gy", outside)
    first = swap(first, "gy", inside)
    state, edges = load_state(acid_field, quencher_field)
    state, edges, second, first = pack_columns(state, edges, second, first)
    inner = swap(first, "gx", inside)
    up = shift(second, "gx", 0)
    state_early, guard = run_main(0, state)
    second, state_early = lax.optimization_barrier((second, state_early))
    down = shift(second, "gx", 1)
    up, inner, state_early = lax.optimization_barrier((up, inner, state_early))
    state, guard = run_main(1, state, state_early, guard)
    strips, guard, density = run_strips(edges, inner, up, down, guard)
    tile = density[:, :TILE]
    pair = jnp.concatenate([tile, swap(tile, "gx", inside)], 1)
    far = swap(pair, "gx", lambda i: i - 2 if i // 2 % 2 == 0 else i + 2)
    near = swap(pair, "gx", lambda i: i ^ 2)
    acid_after, inhibitor, cols = run_last(state, strips, guard)
    near, far, cols = lax.optimization_barrier((near, far, cols))
    mixed = run_mix(pair, near, far, cols)[:, :TILE]
    low = jnp.concatenate([mixed, swap(mixed, "gy", lambda i: i ^ 1)], 1)
    high = swap(low, "gy", lambda i: i ^ 2)
    etch_rate = run_etch(low, high, guard)
    return acid_after, inhibitor, etch_rate


def solution(mesh):
    in_specs = (P(None, "gy", "gx"), P(None, "gy", "gx"))
    out_specs = (P(None, "gy", "gx"), P(None, "gy", "gx"), P("gy", "gx"))
    return jax.shard_map(shards, mesh=mesh, in_specs=in_specs, out_specs=out_specs, check_vma=False)
```
